32 devices in a mesh: seq: 16 (over z, x, core), tp: 2 (over y).
Axes of the slice: x: 2, y: 2, z: 4, core: 2. Of those that a mesh axis runs over, the one named last changes fastest.
Arguments:
- queries: bfloat16 [4096, 4096], P(('seq', 'tp')), may hold values from -6 to 6
- key_states: bfloat16 [4096, 2048], P(('seq', 'tp')), may hold values from -6 to 6
- value_state_rows: bfloat16 [4096, 2048], P(('seq', 'tp')), may hold values from -6 to 6
- out_grad: bfloat16 [4096, 4096], P(('seq', 'tp')), may hold values from -6 to 6
- doc_lengths: int32 [4], replicated, may hold values from 1 to 2048, 4096 in all
Outputs:
- query_grad: bfloat16 [4096, 4096], P(('seq', 'tp'))
- key_gradient: bfloat16 [4096, 2048], P(('seq', 'tp'))
- value_gradient: bfloat16 [4096, 2048], P(('seq', 'tp'))
The draws below stay inside these ranges and needn't reach their ends.
Inputs may be any that keep to these rules, and one draw needn't show every extreme that they name: `doc_lengths`: the documents lie one after another from position 0 and fill all 4096 positions; the longest has exactly 2048 tokens.
All inputs are finite; a program needn't handle non-finite values.
Results may differ from the reference program's by a relative error of at most 0.013.
Values may be sent and summed in bfloat16 or wider, within the bound.
No kernel may reach another device: no remote copies, remote signals or barrier semaphores. Data moves between devices by JAX's collectives and lax.ppermute only.
A program may use at most 64 MiB of HBM per device.

```python
import math
import jax
import jax.numpy as jnp
import numpy as np
from jax import lax

QUERY_HEADS = 32
KEY_HEADS = 16
HEAD_SIZE = 128
WINDOW = 1024
TOK_DEV = 256
PACKED_TOKENS = 4096
DOCS = 4
MOST_DOC = 2048


def draw_queries(key, part):
    random_seed_key = jax.random.fold_in(key, 1)
    value_results = jnp.clip(jax.random.normal(random_seed_key, (PACKED_TOKENS, QUERY_HEADS * HEAD_SIZE)), -5.0, 5.0)
    return value_results.astype(jnp.float32).astype(jnp.bfloat16)


def draw_key_states(key, part):
    random_seed_key = jax.random.fold_in(key, 3)
    value_results = jnp.clip(jax.random.normal(random_seed_key, (PACKED_TOKENS, KEY_HEADS * HEAD_SIZE)), -5.0, 5.0)
    return value_results.astype(jnp.float32).astype(jnp.bfloat16)


def steps_of(stream_key, dims, split, least, largest):
    level = 1.0
    for axis_at, blocks in split:
        draws = jax.random.uniform(jax.random.fold_in(jax.random.fold_in(stream_key, 6), axis_at), (blocks,), jnp.float32, least / len(split), largest / len(split))
        level = level * jnp.repeat(jnp.exp(draws), dims[axis_at] // blocks).reshape((-1,) + (1,) * (len(dims) - 1 - axis_at))
    return level


def split_up(amount, total, bound, skew):
    loads = [(1 << 20) // math.isqrt(grade ** skew) + 1 for grade in range(2, amount + 1)]
    spare, holding = total - bound - (amount - 1), [1] * (amount - 1)
    while spare > 0:
        free = [i for i in range(amount - 1) if holding[i] < bound]
        pool, remaining = sum([loads[i] for i in free]), spare
        for i in free:
            extra = min(bound - holding[i], max(1, remaining * loads[i] // pool), spare)
            holding[i] = holding[i] + extra
            spare = spare - extra
    return np.array([bound] + holding)


def uneven_parts(own_key, amount, total, bound, lean):
    if amount == 2:
        one = jax.random.randint(own_key, (), max(1, total - bound), min(bound, total - 1) + 1)
        return jnp.stack([one, total - one])
    lengths = jnp.asarray(split_up(amount, total, bound, lean), jnp.int32)
    pairs = (amount - 1) // 2
    giver, receiver = lengths[1:1 + 2 * pairs:2], lengths[2:2 + 2 * pairs:2]
    slack = jnp.minimum(giver - 1, bound - receiver)
    passed = jax.random.randint(jax.random.fold_in(own_key, 1), (pairs,), 0, 1 << 20) % (slack + 1)
    lengths = lengths.at[1:1 + 2 * pairs:2].set(giver - passed).at[2:2 + 2 * pairs:2].set(receiver + passed)
    return lengths[jax.random.permutation(jax.random.fold_in(own_key, 2), amount)]


def scatter_about(rng, extent, width, reach, pieces=(), kind=jnp.bfloat16):
    gain = steps_of(rng, extent, pieces, -0.22, 0.18) if pieces else 1.0
    drawn = jax.random.normal(rng, extent, jnp.float32) * width * gain
    return jnp.minimum(jnp.maximum(drawn, -reach), reach).astype(kind)


def setup_inputs(seed: int = 0) -> dict:
    keys = jax.random.split(jax.random.key(seed), 6)
    queries = draw_queries(jax.random.fold_in(keys[5], 71), 0)
    key_states = draw_key_states(jax.random.fold_in(keys[5], 71), 0)
    value_state_rows = scatter_about(keys[2], (PACKED_TOKENS, KEY_HEADS * HEAD_SIZE), 1.0, 6.0, ((0, 32),))
    out_grad = scatter_about(keys[3], (PACKED_TOKENS, QUERY_HEADS * HEAD_SIZE), 1.0, 6.0, ((0, 32),))
    doc_lengths = uneven_parts(keys[4], DOCS, PACKED_TOKENS, MOST_DOC, 2).astype(jnp.int32)
    return dict(queries=queries, key_states=key_states, value_state_rows=value_state_rows, out_grad=out_grad, doc_lengths=doc_lengths)


attn_scale = 168.0 ** -0.5
masked_floor = -1.0e30


def doc_index(starts_arr, positions):
    counted = jnp.sum((starts_arr[None, :] <= positions[:, None]).astype(jnp.int32), axis=1)
    return counted.astype(jnp.int32) - 1


def reference(queries, key_states, value_state_rows, out_grad, doc_lengths):
    group_width = QUERY_HEADS // KEY_HEADS
    key_span = TOK_DEV + WINDOW
    block_count = PACKED_TOKENS // TOK_DEV
    starts_arr = (jnp.cumsum(doc_lengths) - doc_lengths).astype(jnp.int32)

    def head_slices(kv_head):
        zero_pad = jnp.zeros((WINDOW, HEAD_SIZE), jnp.bfloat16)
        key_cols = lax.dynamic_slice_in_dim(key_states, kv_head * HEAD_SIZE, HEAD_SIZE, 1)
        value_cols = lax.dynamic_slice_in_dim(value_state_rows, kv_head * HEAD_SIZE, HEAD_SIZE, 1)
        key_padded = jnp.concatenate([zero_pad, key_cols], axis=0)
        value_padded = jnp.concatenate([zero_pad, value_cols], axis=0)
        query_cols = lax.dynamic_slice_in_dim(queries, kv_head * group_width * HEAD_SIZE, group_width * HEAD_SIZE, 1)
        grad_cols = lax.dynamic_slice_in_dim(out_grad, kv_head * group_width * HEAD_SIZE, group_width * HEAD_SIZE, 1)

        def step(carried, block_index):
            key_grad_pad, value_grad_pad = carried
            query_start = (block_index * TOK_DEV).astype(jnp.int32)
            key_tile = lax.dynamic_slice_in_dim(key_padded, query_start, key_span, 0)
            value_tile = lax.dynamic_slice_in_dim(value_padded, query_start, key_span, 0)
            query_rows = lax.dynamic_slice_in_dim(query_cols, query_start, TOK_DEV, 0)
            grad_rows = lax.dynamic_slice_in_dim(grad_cols, query_start, TOK_DEV, 0)
            query_pos = query_start + jnp.arange(TOK_DEV, dtype=jnp.int32)
            key_pos = query_start - WINDOW + jnp.arange(key_span, dtype=jnp.int32)
            allowed = (key_pos[None, :] <= query_pos[:, None]) & (query_pos[:, None] - key_pos[None, :] < WINDOW)
            allowed = allowed & (key_pos[None, :] >= 0)
            allowed = allowed & (doc_index(starts_arr, key_pos)[None, :] == doc_index(starts_arr, query_pos)[:, None])
            key_acc = jnp.zeros((key_span, HEAD_SIZE), jnp.float32)
            value_acc = jnp.zeros((key_span, HEAD_SIZE), jnp.float32)
            query_parts = []
            for member in range(group_width):
                query_block = query_rows[:, member * HEAD_SIZE:(member + 1) * HEAD_SIZE]
                grad_block = grad_rows[:, member * HEAD_SIZE:(member + 1) * HEAD_SIZE]
                raw_scores = jnp.dot(query_block, key_tile.T, preferred_element_type=jnp.float32) * attn_scale
                row_max = jnp.max(jnp.where(allowed, raw_scores, masked_floor), axis=1)
                row_sum = jnp.sum(jnp.where(allowed, jnp.exp(raw_scores - row_max[:, None]), 0.0), axis=1)
                log_total = row_max + jnp.log(row_sum)
                probs = jnp.where(allowed, jnp.exp(raw_scores - log_total[:, None]), 0.0)
                probs_bf = probs.astype(jnp.bfloat16)
                attn_out = jnp.dot(probs_bf, value_tile, preferred_element_type=jnp.float32)
                delta_rows = jnp.sum(grad_block.astype(jnp.float32) * attn_out, axis=1)
                prob_grad = jnp.dot(grad_block, value_tile.T, preferred_element_type=jnp.float32)
                grad_scores = (probs * (prob_grad - delta_rows[:, None]) * attn_scale).astype(jnp.bfloat16)
                query_parts.append(jnp.dot(grad_scores, key_tile, preferred_element_type=jnp.float32).astype(jnp.bfloat16))
                key_acc = key_acc + jnp.dot(grad_scores.T, query_block, preferred_element_type=jnp.float32)
                value_acc = value_acc + jnp.dot(probs_bf.T, grad_block, preferred_element_type=jnp.float32)
            key_grad_pad = lax.dynamic_update_slice_in_dim(
                key_grad_pad, lax.dynamic_slice_in_dim(key_grad_pad, query_start, key_span, 0) + key_acc, query_start, 0)
            value_grad_pad = lax.dynamic_update_slice_in_dim(
                value_grad_pad, lax.dynamic_slice_in_dim(value_grad_pad, query_start, key_span, 0) + value_acc, query_start, 0)
            return (key_grad_pad, value_grad_pad), jnp.concatenate(query_parts, axis=1)

        start_pad = jnp.zeros((PACKED_TOKENS + WINDOW, HEAD_SIZE), jnp.float32)
        (key_grad_pad, value_grad_pad), query_blocks = lax.scan(
            step, (start_pad, start_pad), jnp.arange(block_count, dtype=jnp.int32))
        query_part = query_blocks.reshape(PACKED_TOKENS, group_width * HEAD_SIZE)
        return query_part, key_grad_pad[WINDOW:].astype(jnp.bfloat16), value_grad_pad[WINDOW:].astype(jnp.bfloat16)

    query_matrix, key_matrix, value_matrix = lax.map(head_slices, jnp.arange(KEY_HEADS, dtype=jnp.int32))
    query_grad = jnp.transpose(query_matrix, (1, 0, 2)).reshape(PACKED_TOKENS, QUERY_HEADS * HEAD_SIZE)
    key_gradient = jnp.transpose(key_matrix, (1, 0, 2)).reshape(PACKED_TOKENS, KEY_HEADS * HEAD_SIZE)
    value_gradient = jnp.transpose(value_matrix, (1, 0, 2)).reshape(PACKED_TOKENS, KEY_HEADS * HEAD_SIZE)
    return (query_grad, key_gradient, value_gradient)
```

```python
import functools
import math

import jax
import jax.numpy as jnp
from jax import lax
from jax.experimental import pallas as pl
from jax.experimental.pallas import tpu as pltpu
from jax.sharding import PartitionSpec as P

QUERY_HEADS = 32
KEY_HEADS = 16
HEAD_SIZE = 128
WINDOW = 1024
GROUP = QUERY_HEADS // KEY_HEADS
AXES = ("seq", "tp")

attn_scale = 168.0 ** (-0.5)
masked_floor = -1e30

CHUNKS = 2
ANY = pl.BlockSpec(memory_space=pl.ANY)
VMEM = pl.BlockSpec(memory_space=pltpu.VMEM)
SMEM = pl.BlockSpec(memory_space=pltpu.SMEM)


class Plan:
    def __init__(self, rows):
        self.seq, self.tp = lax.axis_size("seq"), lax.axis_size("tp")
        self.rows = rows
        self.block = rows * self.tp
        self.slab = WINDOW // self.block
        self.cores = min(2, self.slab)
        self.ways = self.slab // self.cores
        self.groups = self.ways * self.tp
        self.key_heads = KEY_HEADS // self.groups
        self.chunks = min(CHUNKS, self.key_heads)
        self.heads = self.key_heads // self.chunks
        self.key_cols = self.heads * HEAD_SIZE
        self.query_cols = self.key_cols * GROUP
        self.pieces = self.slab * self.tp

    def place(self):
        seq, tp = lax.axis_index("seq"), lax.axis_index("tp")
        inner = lax.rem(seq, self.slab)
        core = lax.rem(inner, self.cores)
        return seq - inner, core, (inner // self.cores) * self.tp + tp

    def routes(self, move):
        pairs = []
        for seq in range(self.seq):
            for tp in range(self.tp):
                slab, inner = divmod(seq, self.slab)
                way, core = divmod(inner, self.cores)
                to = move(slab, core, way * self.tp + tp)
                if to is not None and 0 <= to[0] < self.seq // self.slab:
                    target = (to[0] * self.slab + (to[2] // self.tp) * self.cores + to[1]) * self.tp + to[2] % self.tp
                    pairs.append((seq * self.tp + tp, target))
        return pairs

    def to_group(self, value, flip):
        return lax.ppermute(value, AXES, self.routes(lambda slab, core, group: (slab, core, group ^ flip)))

    def to_core(self, value):
        return lax.ppermute(value, AXES, self.routes(lambda slab, core, group: (slab, self.cores - 1 - core, group)))

    def to_slab(self, value, step):
        return lax.ppermute(value, AXES, self.routes(lambda slab, core, group: (slab + step, core, group)))


def run_copies(copies):
    for copy in copies:
        copy.start()
    for copy in copies:
        copy.wait()


def traffic(count):
    return pl.CostEstimate(flops=0, bytes_accessed=count, transcendentals=0)


def columns(start, width):
    return pl.ds(pl.multiple_of(start, HEAD_SIZE), width)


def split_columns(plan, arrays, width, chunks, name):
    chunk_width = width // chunks

    def kernel(*refs):
        sources, targets, sem = refs[: len(arrays)], refs[len(arrays) : -1], refs[-1]
        _, _, group = plan.place()
        copies = []
        for chunk in range(chunks):
            for flip in range(plan.groups):
                start = (group ^ flip) * width + chunk * chunk_width
                for index, source in enumerate(sources):
                    copies.append(
                        pltpu.make_async_copy(
                            source.at[:, columns(start, chunk_width)],
                            targets[chunk * plan.groups + flip].at[index],
                            sem.at[len(copies)],
                        )
                    )
        run_copies(copies)

    count = chunks * plan.groups
    shape = jax.ShapeDtypeStruct((len(arrays), plan.rows, chunk_width), jnp.bfloat16)
    out = pl.pallas_call(
        kernel,
        out_shape=[shape] * count,
        in_specs=[ANY] * len(arrays),
        out_specs=[VMEM] * count,
        scratch_shapes=[pltpu.SemaphoreType.DMA((count * len(arrays),))],
        cost_estimate=traffic(2 * sum(array.nbytes for array in arrays)),
        name=name,
    )(*arrays)
    return [out[chunk * plan.groups : (chunk + 1) * plan.groups] for chunk in range(chunks)]


def gather_pieces(plan, pieces):
    def kernel(*refs):
        sources, target, sem = refs[:-2], refs[-2], refs[-1]
        _, _, group = plan.place()
        run_copies(
            [pltpu.make_async_copy(source, target.at[group ^ flip], sem.at[flip]) for flip, source in enumerate(sources)]
        )

    return pl.pallas_call(
        kernel,
        out_shape=jax.ShapeDtypeStruct((plan.groups,) + pieces[0].shape, jnp.bfloat16),
        in_specs=[ANY] * plan.groups,
        out_specs=VMEM,
        scratch_shapes=[pltpu.SemaphoreType.DMA((plan.groups,))],
        cost_estimate=traffic(2 * sum(piece.nbytes for piece in pieces)),
        name="gather_keys",
    )(*pieces)


def join_columns(plan, chunked, count, width, name):
    chunks = len(chunked)
    chunk_width = width // chunks
    flat = [piece for pieces in chunked for piece in pieces]

    def kernel(*refs):
        sources, targets, sem = refs[: len(flat)], refs[len(flat) : -1], refs[-1]
        _, _, group = plan.place()
        copies = []
        for chunk in range(chunks):
            for flip in range(plan.groups):
                start = (group ^ flip) * width + chunk * chunk_width
                for index, target in enumerate(targets):
                    copies.append(
                        pltpu.make_async_copy(
                            sources[chunk * plan.groups + flip].at[index],
                            target.at[:, columns(start, chunk_width)],
                            sem.at[len(copies)],
                        )
                    )
        run_copies(copies)

    return pl.pallas_call(
        kernel,
        out_shape=[jax.ShapeDtypeStruct((plan.rows, width * plan.groups), jnp.bfloat16)] * count,
        in_specs=[ANY] * len(flat),
        out_specs=[VMEM] * count,
        scratch_shapes=[pltpu.SemaphoreType.DMA((len(flat) * count,))],
        cost_estimate=traffic(2 * sum(piece.nbytes for piece in flat)),
        name=name,
    )(*flat)


def backward(plan, chunk, doc_lengths, query_pieces, own, own_other, before, before_other):
    tiles = plan.slab + 1
    block, groups, tp, cores = plan.block, plan.groups, plan.tp, plan.cores
    wide = GROUP * block
    exponent_scale = attn_scale * math.log2(math.e)

    def kernel(docs, *refs):
        pieces = refs[:groups]
        key_refs = refs[groups : groups + 4]
        refs = refs[groups + 4 :]
        query_out, refs = refs[:groups], refs[groups:]
        own_mine, own_far, before_mine, before_far = refs[:4]
        q_s, o_s, k_s, v_s, dq_s, dk_s, dv_s, score_s, prob_grad_s, sem = refs[4:]
        slab_seq, core, group = plan.place()

        copies = []

        def add(source, target):
            copies.append(pltpu.make_async_copy(source, target, sem.at[len(copies)]))

        for flip, piece in enumerate(pieces):
            add(piece.at[0], q_s.at[group ^ flip])
            add(piece.at[1], o_s.at[group ^ flip])
        cols = pl.ds(chunk * plan.key_cols, plan.key_cols)
        for source, late, far in zip(key_refs, (1, 1, 0, 0), (0, 1, 0, 1)):
            side = core + far * (cores - 1 - 2 * core)
            for way in range(plan.ways):
                start = late * plan.pieces + (way * cores + side) * tp
                for index, target in enumerate((k_s, v_s)):
                    add(source.at[pl.ds(way * tp, tp), index, :, cols], target.at[pl.ds(start, tp)])
        for copy in copies:
            copy.start()
        dk_s[...] = jnp.zeros_like(dk_s)
        dv_s[...] = jnp.zeros_like(dv_s)
        for copy in copies:
            copy.wait()

        def step(index, carry):
            head, way = index // plan.ways, lax.rem(index, plan.ways)
            key_at = (way * cores + core) * tp
            key_cols = columns(head * HEAD_SIZE, HEAD_SIZE)
            rows_at = pl.ds(way * tp, tp)

            def both(ref):
                parts = [
                    ref[rows_at, :, columns((head * GROUP + member) * HEAD_SIZE, HEAD_SIZE)].reshape(block, HEAD_SIZE)
                    for member in range(GROUP)
                ]
                return jnp.concatenate(parts, axis=0)

            queries, grads = both(q_s), both(o_s)
            inner = lax.broadcasted_iota(jnp.int32, (1, block), 1)
            inner = jnp.concatenate([inner] * GROUP, axis=1)
            first = (slab_seq + way * cores + core) * block
            position = inner + first
            lowest = position - (WINDOW - 1)
            start = jnp.int32(0)
            for doc in range(docs.shape[0]):
                lowest = jnp.where(position >= start, jnp.maximum(lowest, start), lowest)
                start = start + docs[doc]
            lowest = lowest - (first - WINDOW)

            def key_rows(ref, tile):
                return ref[pl.ds(key_at + tile * tp, tp), :, key_cols].reshape(block, HEAD_SIZE)

            def tile_rows(tile):
                return pl.ds(tile * block, block)

            peak = jnp.full((1, wide), masked_floor, jnp.float32)
            for tile in range(tiles):
                scores = lax.dot_general(
                    key_rows(k_s, tile), queries, (((1,), (1,)), ((), ())), preferred_element_type=jnp.float32
                )
                row = lax.broadcasted_iota(jnp.int32, (block, wide), 0)
                allowed = row >= lowest - tile * block
                if tile == tiles - 1:
                    allowed = allowed & (row <= inner)
                scores = jnp.where(allowed, scores, masked_floor)
                peak = jnp.maximum(peak, jnp.max(scores, axis=0, keepdims=True))
                score_s[tile_rows(tile), :] = scores
            peak = peak * exponent_scale
            total = jnp.zeros((1, wide), jnp.float32)
            delta = jnp.zeros((1, wide), jnp.float32)
            for tile in range(tiles):
                raised = jnp.exp2(score_s[tile_rows(tile), :] * exponent_scale - peak)
                prob_grad = lax.dot_general(
                    key_rows(v_s, tile), grads, (((1,), (1,)), ((), ())), preferred_element_type=jnp.float32
                )
                total = total + jnp.sum(raised, axis=0, keepdims=True)
                delta = delta + jnp.sum(raised * prob_grad, axis=0, keepdims=True)
                score_s[tile_rows(tile), :] = raised
                prob_grad_s[tile_rows(tile), :] = prob_grad
            inverse = 1.0 / total
            delta = delta * inverse
            query_sum = jnp.zeros((HEAD_SIZE, wide), jnp.float32)
            for tile in range(tiles):
                probs = score_s[tile_rows(tile), :] * inverse
                grad_scores = (probs * (prob_grad_s[tile_rows(tile), :] - delta) * attn_scale).astype(jnp.bfloat16)
                at = pl.ds(key_at + tile * tp, tp)
                value_part = jnp.dot(probs.astype(jnp.bfloat16), grads, preferred_element_type=jnp.float32)
                dv_s[at, :, key_cols] += value_part.reshape(tp, plan.rows, HEAD_SIZE)
                key_part = jnp.dot(grad_scores, queries, preferred_element_type=jnp.float32)
                dk_s[at, :, key_cols] += key_part.reshape(tp, plan.rows, HEAD_SIZE)
                query_sum += lax.dot_general(
                    key_rows(k_s, tile), grad_scores, (((0,), (0,)), ((), ())), preferred_element_type=jnp.float32
                )
            query_rows = query_sum.T.astype(jnp.bfloat16)
            for member in range(GROUP):
                dq_s[rows_at, :, columns((head * GROUP + member) * HEAD_SIZE, HEAD_SIZE)] = query_rows[
                    member * block : (member + 1) * block
                ].reshape(tp, plan.rows, HEAD_SIZE)
            return carry

        lax.fori_loop(0, plan.heads * plan.ways, step, 0)
        for flip in range(groups):
            query_out[flip][0] = dq_s[group ^ flip]
        for late, far, target in ((1, 0, own_mine), (1, 1, own_far), (0, 0, before_mine), (0, 1, before_far)):
            side = core + far * (cores - 1 - 2 * core)
            for way in range(plan.ways):
                at = pl.ds(late * plan.pieces + (way * cores + side) * tp, tp)
                for index, source in enumerate((dk_s, dv_s)):
                    target[pl.ds(way * tp, tp), index] = source[at].astype(target.dtype)

    part = (groups, 2, plan.rows, plan.key_cols)
    bf, fl = jnp.bfloat16, jnp.float32
    span = 2 * plan.pieces
    pairs = tiles * block * wide * plan.heads * plan.ways
    out = pl.pallas_call(
        kernel,
        out_shape=[jax.ShapeDtypeStruct((1, plan.rows, plan.query_cols), bf)] * groups
        + [jax.ShapeDtypeStruct(part, dtype) for dtype in (fl, bf, fl, bf)],
        in_specs=[SMEM] + [ANY] * (groups + 4),
        out_specs=[VMEM] * (groups + 4),
        scratch_shapes=[
            pltpu.VMEM((groups, plan.rows, plan.query_cols), bf),
            pltpu.VMEM((groups, plan.rows, plan.query_cols), bf),
            pltpu.VMEM((span, plan.rows, plan.key_cols), bf),
            pltpu.VMEM((span, plan.rows, plan.key_cols), bf),
            pltpu.VMEM((groups, plan.rows, plan.query_cols), bf),
            pltpu.VMEM((span, plan.rows, plan.key_cols), fl),
            pltpu.VMEM((span, plan.rows, plan.key_cols), fl),
            pltpu.VMEM((tiles * block, wide), fl),
            pltpu.VMEM((tiles * block, wide), fl),
            pltpu.SemaphoreType.DMA((2 * groups + 8 * plan.ways,)),
        ],
        compiler_params=pltpu.CompilerParams(vmem_limit_bytes=40 * 1024 * 1024),
        cost_estimate=pl.CostEstimate(flops=10 * pairs * HEAD_SIZE, bytes_accessed=6 << 20, transcendentals=pairs),
        name="backward",
    )(doc_lengths, *query_pieces, own, own_other, before, before_other)
    return out[:groups], out[groups:]


def add_up(plan, mine, far, later):
    def kernel(mine_ref, far_ref, later_ref, *targets):
        _, _, group = plan.place()
        for flip, target in enumerate(targets):
            at = group ^ flip
            total = mine_ref[at] + far_ref[at].astype(jnp.float32) + later_ref[at].astype(jnp.float32)
            target[...] = total.astype(jnp.bfloat16)

    shape = jax.ShapeDtypeStruct(mine.shape[1:], jnp.bfloat16)
    return pl.pallas_call(
        kernel,
        out_shape=[shape] * plan.groups,
        in_specs=[VMEM] * 3,
        out_specs=[VMEM] * plan.groups,
        cost_estimate=traffic(mine.nbytes + far.nbytes * 3),
        name="add_up",
    )(mine, far, later)


def per_device(queries, key_states, value_state_rows, out_grad, doc_lengths):
    plan = Plan(queries.shape[0])
    key_width = KEY_HEADS * HEAD_SIZE // plan.groups
    query_width = QUERY_HEADS * HEAD_SIZE // plan.groups

    def exchange(pieces):
        return [pieces[0]] + [plan.to_group(pieces[flip], flip) for flip in range(1, plan.groups)]

    key_pieces = exchange(split_columns(plan, (key_states, value_state_rows), key_width, 1, "split_keys")[0])
    query_chunks = split_columns(plan, (queries, out_grad), query_width, plan.chunks, "split_queries")
    key_pieces, query_chunks = lax.optimization_barrier((key_pieces, query_chunks))
    own = gather_pieces(plan, key_pieces)
    before = plan.to_slab(own, 1)
    own_other = plan.to_core(own)
    arrived = [exchange(query_chunks[0])]
    before, own_other, arrived[0] = lax.optimization_barrier((before, own_other, arrived[0]))
    before_other = plan.to_core(before)
    for chunk in range(1, plan.chunks):
        arrived.append(exchange(query_chunks[chunk]))
    query_results, key_results = [], []
    for chunk in range(plan.chunks):
        pieces = arrived[chunk]
        query_out, (own_mine, own_far, before_mine, before_far) = backward(
            plan, chunk, doc_lengths, pieces, own, own_other, before, before_other
        )
        before_sum = (before_mine + plan.to_core(before_far).astype(jnp.float32)).astype(jnp.bfloat16)
        later = plan.to_slab(before_sum, -1)
        far = plan.to_core(own_far)
        query_results.append(exchange(query_out))
        key_results.append(exchange(add_up(plan, own_mine, far, later)))
    (query_grad,) = join_columns(plan, query_results, 1, query_width, "join_queries")
    key_gradient, value_gradient = join_columns(plan, key_results, 2, key_width, "join_keys")
    return query_grad, key_gradient, value_gradient


def solution(mesh):
    split = P(("seq", "tp"), None)
    return jax.shard_map(
        per_device,
        mesh=mesh,
        in_specs=(split, split, split, split, P()),
        out_specs=(split, split, split),
        check_vma=False,
    )
```

```python
import itertools
import math

import jax
import jax.numpy as jnp
from jax import lax
from jax.experimental import pallas as pl
from jax.experimental.pallas import tpu as pltpu
from jax.sharding import PartitionSpec as P

QUERY_HEADS = 32
KEY_HEADS = 16
HEAD_SIZE = 128
WINDOW = 1024
GROUP = QUERY_HEADS // KEY_HEADS
AXES = ("seq", "tp")

attn_scale = 168.0 ** (-0.5)
masked_floor = -1e30

CHUNKS = 2
VMEM_LIMIT = 56 * 1024 * 1024
ANY = pl.BlockSpec(memory_space=pl.ANY)
VMEM = pl.BlockSpec(memory_space=pltpu.VMEM)
SMEM = pl.BlockSpec(memory_space=pltpu.SMEM)


class Plan:
    def __init__(self, rows):
        self.seq, self.tp = lax.axis_size("seq"), lax.axis_size("tp")
        self.rows = rows
        self.block = rows * self.tp
        self.slab = WINDOW // self.block
        self.cores = min(2, self.slab)
        self.ways = self.slab // self.cores
        self.groups = self.ways * self.tp
        self.key_heads = KEY_HEADS // self.groups
        self.chunks = min(CHUNKS, self.key_heads)
        self.heads = self.key_heads // self.chunks
        self.key_cols = self.heads * HEAD_SIZE
        self.query_cols = self.key_cols * GROUP
        self.pieces = self.slab * self.tp

    def place(self):
        seq, tp = lax.axis_index("seq"), lax.axis_index("tp")
        inner = lax.rem(seq, self.slab)
        core = lax.rem(inner, self.cores)
        return seq - inner, core, (inner // self.cores) * self.tp + tp

    def routes(self, move):
        pairs = []
        for seq in range(self.seq):
            for tp in range(self.tp):
                slab, inner = divmod(seq, self.slab)
                way, core = divmod(inner, self.cores)
                to_slab, to_core, to_group = move(slab, core, way * self.tp + tp)
                to_slab %= self.seq // self.slab
                target = (to_slab * self.slab + to_group // self.tp * self.cores + to_core) * self.tp + to_group % self.tp
                pairs.append((seq * self.tp + tp, target))
        return pairs

    def to_group(self, value, flip):
        return lax.ppermute(value, AXES, self.routes(lambda slab, core, group: (slab, core, group ^ flip)))

    def to_core(self, value):
        return lax.ppermute(value, AXES, self.routes(lambda slab, core, group: (slab, self.cores - 1 - core, group)))

    def to_slab(self, value, step):
        return lax.ppermute(value, AXES, self.routes(lambda slab, core, group: (slab + step, core, group)))


def run_copies(copies):
    for copy in copies:
        copy.start()
    for copy in copies:
        copy.wait()


def traffic(count):
    return pl.CostEstimate(flops=0, bytes_accessed=count, transcendentals=0)


def columns(start, width):
    return pl.ds(pl.multiple_of(start, HEAD_SIZE), width)


def split_columns(plan, arrays, width, chunks, name, after=()):
    chunk_width = width // chunks

    def kernel(*refs):
        sources, targets, sem = refs[: len(arrays)], refs[len(arrays) + len(after) : -1], refs[-1]
        _, _, group = plan.place()
        copies = []
        for chunk in range(chunks):
            for flip in range(plan.groups):
                start = (group ^ flip) * width + chunk * chunk_width
                for index, source in enumerate(sources):
                    copies.append(
                        pltpu.make_async_copy(
                            source.at[:, columns(start, chunk_width)],
                            targets[chunk * plan.groups + flip].at[index],
                            sem.at[len(copies)],
                        )
                    )
        run_copies(copies)

    count = chunks * plan.groups
    shape = jax.ShapeDtypeStruct((len(arrays), plan.rows, chunk_width), jnp.bfloat16)
    out = pl.pallas_call(
        kernel,
        out_shape=[shape] * count,
        in_specs=[ANY] * (len(arrays) + len(after)),
        out_specs=[VMEM] * count,
        scratch_shapes=[pltpu.SemaphoreType.DMA((count * len(arrays),))],
        cost_estimate=traffic(2 * sum(array.nbytes for array in arrays)),
        name=name,
    )(*arrays, *after)
    return [out[chunk * plan.groups : (chunk + 1) * plan.groups] for chunk in range(chunks)]


def join_columns(plan, chunked, count, width, name):
    chunks = len(chunked)
    chunk_width = width // chunks
    flat = [piece for pieces in chunked for piece in pieces]

    def kernel(*refs):
        sources, targets, sem = refs[: len(flat)], refs[len(flat) : -1], refs[-1]
        _, _, group = plan.place()
        copies = []
        for chunk in range(chunks):
            for flip in range(plan.groups):
                start = (group ^ flip) * width + chunk * chunk_width
                for index, target in enumerate(targets):
                    copies.append(
                        pltpu.make_async_copy(
                            sources[chunk * plan.groups + flip].at[index],
                            target.at[:, columns(start, chunk_width)],
                            sem.at[len(copies)],
                        )
                    )
        run_copies(copies)

    return pl.pallas_call(
        kernel,
        out_shape=[jax.ShapeDtypeStruct((plan.rows, width * plan.groups), jnp.bfloat16)] * count,
        in_specs=[ANY] * len(flat),
        out_specs=[VMEM] * count,
        scratch_shapes=[pltpu.SemaphoreType.DMA((len(flat) * count,))],
        cost_estimate=traffic(2 * sum(piece.nbytes for piece in flat)),
        name=name,
    )(*flat)


def backward(plan, chunk, first_head, heads, doc_lengths, query_pieces, key_pieces, earlier, after):
    tiles = plan.slab + 1
    block, groups, tp, cores = plan.block, plan.groups, plan.tp, plan.cores
    wide = GROUP * block
    query_width = HEAD_SIZE * GROUP
    key_cols, query_cols = heads * HEAD_SIZE, heads * query_width
    done_cols = first_head * query_width
    exponent_scale = attn_scale * math.log2(math.e)

    def kernel(docs, *refs):
        pieces, refs = refs[:groups], refs[groups:]
        key_refs, refs = refs[: 4 * groups], refs[4 * groups :]
        done, refs = refs[: len(earlier)], refs[len(earlier) + len(after) :]
        query_out, refs = refs[:groups], refs[groups:]
        mine, far, q_s, o_s, k_s, v_s, dq_s, dk_s, dv_s, score_s, prob_grad_s, prob_s, grad_s, sem = refs
        slab_seq, core, group = plan.place()

        copies = []

        def add(source, target):
            copies.append(pltpu.make_async_copy(source, target, sem.at[len(copies)]))

        for flip, piece in enumerate(pieces):
            add(piece.at[0, :, pl.ds(done_cols, query_cols)], q_s.at[group ^ flip])
            add(piece.at[1, :, pl.ds(done_cols, query_cols)], o_s.at[group ^ flip])
        cols = pl.ds((chunk * plan.heads + first_head) * HEAD_SIZE, key_cols)
        for source, (late, away, flip) in zip(key_refs, itertools.product((1, 0), (0, 1), range(groups))):
            side = core + away * (cores - 1 - 2 * core)
            way, lane = (group ^ flip) // tp, lax.rem(group ^ flip, tp)
            start = late * plan.pieces + (way * cores + side) * tp + lane
            for index, target in enumerate((k_s, v_s)):
                add(source.at[index, :, cols], target.at[start])
        for source, target in zip(done, query_out):
            add(source.at[0, :, pl.ds(0, done_cols)], target.at[0, :, pl.ds(0, done_cols)])
        for copy in copies:
            copy.start()
        dk_s[...] = jnp.zeros_like(dk_s)
        dv_s[...] = jnp.zeros_like(dv_s)
        for copy in copies:
            copy.wait()

        def step(index, carry):
            head, way = index // plan.ways, lax.rem(index, plan.ways)
            key_at = (way * cores + core) * tp
            head_cols = columns(head * HEAD_SIZE, HEAD_SIZE)
            rows_at = pl.ds(way * tp, tp)

            def both(ref):
                parts = [
                    ref[rows_at, :, columns((head * GROUP + member) * HEAD_SIZE, HEAD_SIZE)].reshape(block, HEAD_SIZE)
                    for member in range(GROUP)
                ]
                return jnp.concatenate(parts, axis=0)

            queries, grads = both(q_s), both(o_s)
            inner = lax.broadcasted_iota(jnp.int32, (1, block), 1)
            inner = jnp.concatenate([inner] * GROUP, axis=1)
            first = (slab_seq + way * cores + core) * block
            position = inner + first
            lowest = position - (WINDOW - 1)
            start = jnp.int32(0)
            for doc in range(docs.shape[0]):
                lowest = jnp.where(position >= start, jnp.maximum(lowest, start), lowest)
                start = start + docs[doc]
            lowest = lowest - (first - WINDOW)

            def key_rows(ref, tile):
                return ref[pl.ds(key_at + tile * tp, tp), :, head_cols].reshape(block, HEAD_SIZE)

            def tile_rows(tile):
                return pl.ds(tile * block, block)

            peak = jnp.full((1, wide), masked_floor, jnp.float32)
            for tile in range(tiles):
                scores = lax.dot_general(
                    key_rows(k_s, tile), queries, (((1,), (1,)), ((), ())), preferred_element_type=jnp.float32
                )
                row = lax.broadcasted_iota(jnp.int32, (block, wide), 0)
                allowed = row >= lowest - tile * block
                if tile == tiles - 1:
                    allowed = allowed & (row <= inner)
                scores = jnp.where(allowed, scores, masked_floor)
                peak = jnp.maximum(peak, jnp.max(scores, axis=0, keepdims=True))
                score_s[tile_rows(tile), :] = scores
            peak = peak * exponent_scale
            total = jnp.zeros((1, wide), jnp.float32)
            delta = jnp.zeros((1, wide), jnp.float32)
            for tile in range(tiles):
                raised = jnp.exp2(score_s[tile_rows(tile), :] * exponent_scale - peak)
                prob_grad = lax.dot_general(
                    key_rows(v_s, tile), grads, (((1,), (1,)), ((), ())), preferred_element_type=jnp.float32
                )
                total = total + jnp.sum(raised, axis=0, keepdims=True)
                delta = delta + jnp.sum(raised * prob_grad, axis=0, keepdims=True)
                score_s[tile_rows(tile), :] = raised
                prob_grad_s[tile_rows(tile), :] = prob_grad
            inverse = 1.0 / total
            delta = delta * inverse
            for tile in range(tiles):
                probs = score_s[tile_rows(tile), :] * inverse
                prob_s[tile_rows(tile), :] = probs.astype(jnp.bfloat16)
                grad_scores = probs * (prob_grad_s[tile_rows(tile), :] - delta) * attn_scale
                grad_s[tile_rows(tile), :] = grad_scores.astype(jnp.bfloat16)
            at = pl.ds(key_at, tiles * tp)
            shape = (tiles * tp, plan.rows, HEAD_SIZE)
            dv_s[at, :, head_cols] += jnp.dot(prob_s[...], grads, preferred_element_type=jnp.float32).reshape(shape)
            dk_s[at, :, head_cols] += jnp.dot(grad_s[...], queries, preferred_element_type=jnp.float32).reshape(shape)
            query_sum = lax.dot_general(
                k_s[at, :, head_cols].reshape(tiles * block, HEAD_SIZE),
                grad_s[...],
                (((0,), (0,)), ((), ())),
                preferred_element_type=jnp.float32,
            )
            query_rows = query_sum.T.astype(jnp.bfloat16)
            for member in range(GROUP):
                dq_s[rows_at, :, columns((head * GROUP + member) * HEAD_SIZE, HEAD_SIZE)] = query_rows[
                    member * block : (member + 1) * block
                ].reshape(tp, plan.rows, HEAD_SIZE)
            return carry

        lax.fori_loop(0, heads * plan.ways, step, 0)
        for flip in range(groups):
            query_out[flip][0, :, done_cols:] = dq_s[group ^ flip]
        for late, away, piece in itertools.product((0, 1), (0, 1), range(groups)):
            side = core + away * (cores - 1 - 2 * core)
            at = late * plan.pieces + (piece // tp * cores + side) * tp + piece % tp
            for index, source in enumerate((dk_s, dv_s)):
                target = (mine, far)[away]
                target[late, piece, index] = source[at].astype(target.dtype)

    part = (2, groups, 2, plan.rows, key_cols)
    bf, fl = jnp.bfloat16, jnp.float32
    span = 2 * plan.pieces
    pairs = tiles * block * wide * heads * plan.ways
    out = pl.pallas_call(
        kernel,
        out_shape=[jax.ShapeDtypeStruct((1, plan.rows, done_cols + query_cols), bf)] * groups
        + [jax.ShapeDtypeStruct(part, fl), jax.ShapeDtypeStruct(part, bf)],
        in_specs=[SMEM] + [ANY] * (5 * groups + len(earlier) + len(after)),
        out_specs=[VMEM] * (groups + 2),
        scratch_shapes=[
            pltpu.VMEM((groups, plan.rows, query_cols), bf),
            pltpu.VMEM((groups, plan.rows, query_cols), bf),
            pltpu.VMEM((span, plan.rows, key_cols), bf),
            pltpu.VMEM((span, plan.rows, key_cols), bf),
            pltpu.VMEM((groups, plan.rows, query_cols), bf),
            pltpu.VMEM((span, plan.rows, key_cols), fl),
            pltpu.VMEM((span, plan.rows, key_cols), fl),
            pltpu.VMEM((tiles * block, wide), fl),
            pltpu.VMEM((tiles * block, wide), fl),
            pltpu.VMEM((tiles * block, wide), bf),
            pltpu.VMEM((tiles * block, wide), bf),
            pltpu.SemaphoreType.DMA((10 * groups + len(earlier),)),
        ],
        compiler_params=pltpu.CompilerParams(vmem_limit_bytes=VMEM_LIMIT),
        cost_estimate=pl.CostEstimate(flops=160 * pairs * HEAD_SIZE, bytes_accessed=6 << 20, transcendentals=pairs),
        name="backward",
    )(doc_lengths, *query_pieces, *key_pieces, *earlier, *after)
    return out[:groups], out[groups], out[groups + 1]


def half(array, late):
    block = (1,) + array.shape[1:]
    return pl.BlockSpec(block, lambda step: (late,) + (0,) * (len(block) - 1))


def add_before(plan, mine, far, after):
    parts = len(mine)

    def kernel(*refs):
        target = refs[-1]
        at = 0
        for mine_ref, far_ref in zip(refs[:parts], refs[parts : 2 * parts]):
            width = mine_ref.shape[-1]
            total = mine_ref[0] + far_ref[0].astype(jnp.float32)
            target[:, :, :, at : at + width] = total.astype(jnp.bfloat16)
            at += width

    shape = mine[0].shape[1:-1] + (plan.key_cols,)
    return pl.pallas_call(
        kernel,
        grid=(1,),
        out_shape=jax.ShapeDtypeStruct(shape, jnp.bfloat16),
        in_specs=[half(array, 0) for array in (*mine, *far)] + [ANY] * len(after),
        out_specs=pl.BlockSpec(shape, lambda step: (0,) * len(shape)),
        cost_estimate=traffic(8 * math.prod(shape)),
        name="add_before",
    )(*mine, *far, *after)


def add_up(plan, mine, far, later):
    parts = len(mine)

    def kernel(*refs):
        later_ref, targets = refs[2 * parts], refs[2 * parts + 1 :]
        _, _, group = plan.place()
        for flip, target in enumerate(targets):
            piece = group ^ flip
            at = 0
            for mine_ref, far_ref in zip(refs[:parts], refs[parts : 2 * parts]):
                width = mine_ref.shape[-1]
                total = mine_ref[0, piece] + far_ref[0, piece].astype(jnp.float32)
                total = total + later_ref[piece, :, :, at : at + width].astype(jnp.float32)
                target[:, :, at : at + width] = total.astype(jnp.bfloat16)
                at += width

    shape = later.shape[1:]
    return pl.pallas_call(
        kernel,
        grid=(1,),
        out_shape=[jax.ShapeDtypeStruct(shape, jnp.bfloat16)] * plan.groups,
        in_specs=[half(array, 1) for array in (*mine, *far)] + [pl.BlockSpec(later.shape, lambda step: (0,) * later.ndim)],
        out_specs=[pl.BlockSpec(shape, lambda step: (0,) * len(shape))] * plan.groups,
        cost_estimate=traffic(10 * math.prod(later.shape)),
        name="add_up",
    )(*mine, *far, later)


def per_device(queries, key_states, value_state_rows, out_grad, doc_lengths):
    plan = Plan(queries.shape[0])
    key_width = KEY_HEADS * HEAD_SIZE // plan.groups
    query_width = QUERY_HEADS * HEAD_SIZE // plan.groups

    def exchange(pieces):
        return [pieces[0]] + [plan.to_group(pieces[flip], flip) for flip in range(1, plan.groups)]

    key_parts = split_columns(plan, (key_states, value_state_rows), key_width, 1, "split_keys")[0]
    query_chunks = split_columns(
        plan, (queries, out_grad), query_width, plan.chunks, "split_queries", after=(key_parts[0],)
    )
    own = exchange(key_parts)
    arrived = [exchange(parts) for parts in query_chunks]
    before = [plan.to_slab(piece, 1) for piece in own]
    key_pieces = own + [plan.to_core(piece) for piece in own] + before + [plan.to_core(piece) for piece in before]
    query_results, key_results, after = [], [], ()
    for chunk in range(plan.chunks):
        split = chunk > 0 and plan.heads > 1
        calls = [(head, 1) for head in range(plan.heads)] if split else [(0, plan.heads)]
        query_out, mine, far = (), [], []
        for first_head, heads in calls:
            query_out, mine_part, far_part = backward(
                plan, chunk, first_head, heads, doc_lengths, arrived[chunk], key_pieces, query_out, after
            )
            after = (far_part,) if not far and chunk == 0 else after
            mine.append(mine_part)
            far.append(plan.to_core(far_part))
            if split and len(far) == 1:
                after = sent
        before_sum = add_before(plan, mine, far, (later,) if key_results else ())
        later = plan.to_slab(before_sum, -1)
        query_results.append(exchange(query_out))
        key_results.append(exchange(add_up(plan, mine, far, later)))
        sent = (before_sum, *query_results[-1][1:])
    (query_grad,) = join_columns(plan, query_results, 1, query_width, "join_queries")
    key_gradient, value_gradient = join_columns(plan, key_results, 2, key_width, "join_keys")
    return query_grad, key_gradient, value_gradient


def solution(mesh):
    split = P(("seq", "tp"), None)
    return jax.shard_map(
        per_device,
        mesh=mesh,
        in_specs=(split, split, split, split, P()),
        out_specs=(split, split, split),
        check_vma=False,
    )
```

```python
import itertools
import math

import jax
import jax.numpy as jnp
from jax import lax
from jax.experimental import pallas as pl
from jax.experimental.pallas import tpu as pltpu
from jax.sharding import PartitionSpec as P

QUERY_HEADS = 32
KEY_HEADS = 16
HEAD_SIZE = 128
WINDOW = 1024
GROUP = QUERY_HEADS // KEY_HEADS
AXES = ("seq", "tp")

attn_scale = 168.0 ** (-0.5)
masked_floor = -1e30

CHUNKS = 2
EASY, HARD = 1 << 21, 1 << 25
VMEM_LIMIT = 56 * 1024 * 1024
ANY = pl.BlockSpec(memory_space=pl.ANY)
VMEM = pl.BlockSpec(memory_space=pltpu.VMEM)
SMEM = pl.BlockSpec(memory_space=pltpu.SMEM)


class Plan:
    def __init__(self, rows):
        self.seq, self.tp = lax.axis_size("seq"), lax.axis_size("tp")
        self.rows = rows
        self.block = rows * self.tp
        self.slab = WINDOW // self.block
        self.cores = min(2, self.slab)
        self.ways = self.slab // self.cores
        self.groups = self.ways * self.tp
        self.key_heads = KEY_HEADS // self.groups
        self.chunks = min(CHUNKS, self.key_heads)
        self.heads = self.key_heads // self.chunks
        self.key_cols = self.heads * HEAD_SIZE
        self.query_cols = self.key_cols * GROUP
        self.pieces = self.slab * self.tp
        self.flips = sorted(range(self.groups), key=lambda flip: (flip > 0, -bin(flip).count("1")))

    def place(self):
        seq, tp = lax.axis_index("seq"), lax.axis_index("tp")
        inner = lax.rem(seq, self.slab)
        core = lax.rem(inner, self.cores)
        return seq - inner, core, (inner // self.cores) * self.tp + tp

    def routes(self, move):
        pairs = []
        for seq in range(self.seq):
            for tp in range(self.tp):
                slab, inner = divmod(seq, self.slab)
                way, core = divmod(inner, self.cores)
                to_slab, to_core, to_group = move(slab, core, way * self.tp + tp)
                to_slab %= self.seq // self.slab
                target = (to_slab * self.slab + to_group // self.tp * self.cores + to_core) * self.tp + to_group % self.tp
                pairs.append((seq * self.tp + tp, target))
        return pairs

    def to_group(self, value, flip):
        return lax.ppermute(value, AXES, self.routes(lambda slab, core, group: (slab, core, group ^ flip)))

    def to_core(self, value):
        return lax.ppermute(value, AXES, self.routes(lambda slab, core, group: (slab, self.cores - 1 - core, group)))

    def to_slab(self, value, step):
        return lax.ppermute(value, AXES, self.routes(lambda slab, core, group: (slab + step, core, group)))


def run_copies(copies):
    for copy in copies:
        copy.start()
    for copy in copies:
        copy.wait()


def traffic(count):
    return pl.CostEstimate(flops=0, bytes_accessed=count, transcendentals=0)


def columns(start, width):
    return pl.ds(pl.multiple_of(start, HEAD_SIZE), width)


def split_columns(plan, arrays, width, chunks, name, after=()):
    chunk_width = width // chunks

    def kernel(*refs):
        sources, targets, sem = refs[: len(arrays)], refs[len(arrays) + len(after) : -1], refs[-1]
        _, _, group = plan.place()
        copies = []
        for chunk in range(chunks):
            for at, flip in enumerate(plan.flips):
                start = (group ^ flip) * width + chunk * chunk_width
                for index, source in enumerate(sources):
                    copies.append(
                        pltpu.make_async_copy(
                            source.at[:, columns(start, chunk_width)],
                            targets[chunk * plan.groups + at].at[index],
                            sem.at[len(copies)],
                        )
                    )
        run_copies(copies)

    count = chunks * plan.groups
    shape = jax.ShapeDtypeStruct((len(arrays), plan.rows, chunk_width), jnp.bfloat16)
    out = pl.pallas_call(
        kernel,
        out_shape=[shape] * count,
        in_specs=[ANY] * (len(arrays) + len(after)),
        out_specs=[VMEM] * count,
        scratch_shapes=[pltpu.SemaphoreType.DMA((count * len(arrays),))],
        cost_estimate=traffic(2 * sum(array.nbytes for array in arrays)),
        name=name,
    )(*arrays, *after)
    return [out[chunk * plan.groups : (chunk + 1) * plan.groups] for chunk in range(chunks)]


def gather_pieces(plan, pieces, cost, after=()):
    def kernel(*refs):
        sources, target, sem = refs[: plan.groups], refs[-2], refs[-1]
        _, _, group = plan.place()
        run_copies(
            [
                pltpu.make_async_copy(source, target.at[group ^ flip], sem.at[flip])
                for flip, source in zip(plan.flips, sources)
            ]
        )

    return pl.pallas_call(
        kernel,
        out_shape=jax.ShapeDtypeStruct((plan.groups,) + pieces[0].shape, jnp.bfloat16),
        in_specs=[ANY] * (plan.groups + len(after)),
        out_specs=VMEM,
        scratch_shapes=[pltpu.SemaphoreType.DMA((plan.groups,))],
        cost_estimate=traffic(cost),
        name="gather_keys",
    )(*pieces, *after)


def backward(plan, chunk, doc_lengths, query_pieces, key_arrays, after):
    tiles = plan.slab + 1
    block, groups, tp, cores = plan.block, plan.groups, plan.tp, plan.cores
    heads, key_cols, query_cols = plan.heads, plan.key_cols, plan.query_cols
    wide = GROUP * block
    query_width = HEAD_SIZE * GROUP
    exponent_scale = attn_scale * math.log2(math.e)
    loads = heads * (2 * groups + 8 * plan.ways)
    stores = heads * (2 * groups + 3)

    def kernel(docs, *refs):
        pieces, refs = refs[:groups], refs[groups:]
        key_refs, refs = refs[:4], refs[4:]
        refs = refs[len(after) :]
        query_out, refs = refs[:groups], refs[groups:]
        before_mine, own_mine, own_far, refs = *refs[:3], refs[3:]
        parts = (before_mine, None, own_mine, own_far)
        before_far, refs = refs[:groups], refs[groups:]
        q_s, o_s, k_s, v_s, dq_s, dk_s, dv_s, part_s, score_s, prob_grad_s, prob_s, grad_s, sem, out_sem = refs
        slab_seq, core, group = plan.place()

        copies, results = [], []

        def load(source, target):
            copies.append(pltpu.make_async_copy(source, target, sem.at[len(copies)]))
            copies[-1].start()

        def store(source, target):
            results.append(pltpu.make_async_copy(source, target, out_sem.at[len(results)]))
            results[-1].start()

        for head in range(heads):
            here, there = pl.ds(head * query_width, query_width), pl.ds((chunk * heads + head) * query_width, query_width)
            for flip, piece in zip(plan.flips, pieces):
                load(piece.at[0, :, there], q_s.at[group ^ flip, :, here])
                load(piece.at[1, :, there], o_s.at[group ^ flip, :, here])
            here, there = pl.ds(head * HEAD_SIZE, HEAD_SIZE), pl.ds((chunk * heads + head) * HEAD_SIZE, HEAD_SIZE)
            for source, (late, away) in zip(key_refs, itertools.product((1, 0), (0, 1))):
                side = core + away * (cores - 1 - 2 * core)
                for way in range(plan.ways):
                    start = late * plan.pieces + (way * cores + side) * tp
                    for index, target in enumerate((k_s, v_s)):
                        load(source.at[pl.ds(way * tp, tp), index, :, there], target.at[pl.ds(start, tp), :, here])
        dk_s[...] = jnp.zeros_like(dk_s)
        dv_s[...] = jnp.zeros_like(dv_s)

        def step(head, way):
            key_at = (way * cores + core) * tp
            head_cols = pl.ds(head * HEAD_SIZE, HEAD_SIZE)
            rows_at = pl.ds(way * tp, tp)

            def both(ref):
                parts = [
                    ref[rows_at, :, pl.ds((head * GROUP + member) * HEAD_SIZE, HEAD_SIZE)].reshape(block, HEAD_SIZE)
                    for member in range(GROUP)
                ]
                return jnp.concatenate(parts, axis=0)

            queries, grads = both(q_s), both(o_s)
            inner = lax.broadcasted_iota(jnp.int32, (1, block), 1)
            inner = jnp.concatenate([inner] * GROUP, axis=1)
            first = (slab_seq + way * cores + core) * block
            position = inner + first
            lowest = position - (WINDOW - 1)
            start = jnp.int32(0)
            for doc in range(docs.shape[0]):
                lowest = jnp.where(position >= start, jnp.maximum(lowest, start), lowest)
                start = start + docs[doc]
            lowest = lowest - (first - WINDOW)

            def key_rows(ref, tile):
                return ref[pl.ds(key_at + tile * tp, tp), :, head_cols].reshape(block, HEAD_SIZE)

            def tile_rows(tile):
                return pl.ds(tile * block, block)

            peak = jnp.full((1, wide), masked_floor, jnp.float32)
            for tile in range(tiles):
                scores = lax.dot_general(
                    key_rows(k_s, tile), queries, (((1,), (1,)), ((), ())), preferred_element_type=jnp.float32
                )
                row = lax.broadcasted_iota(jnp.int32, (block, wide), 0)
                allowed = row >= lowest - tile * block
                if tile == tiles - 1:
                    allowed = allowed & (row <= inner)
                scores = jnp.where(allowed, scores, masked_floor)
                peak = jnp.maximum(peak, jnp.max(scores, axis=0, keepdims=True))
                score_s[tile_rows(tile), :] = scores
            peak = peak * exponent_scale
            total = jnp.zeros((1, wide), jnp.float32)
            delta = jnp.zeros((1, wide), jnp.float32)
            for tile in range(tiles):
                raised = jnp.exp2(score_s[tile_rows(tile), :] * exponent_scale - peak)
                prob_grad = lax.dot_general(
                    key_rows(v_s, tile), grads, (((1,), (1,)), ((), ())), preferred_element_type=jnp.float32
                )
                total = total + jnp.sum(raised, axis=0, keepdims=True)
                delta = delta + jnp.sum(raised * prob_grad, axis=0, keepdims=True)
                score_s[tile_rows(tile), :] = raised
                prob_grad_s[tile_rows(tile), :] = prob_grad
            inverse = 1.0 / total
            delta = delta * inverse
            for tile in range(tiles):
                probs = score_s[tile_rows(tile), :] * inverse
                prob_s[tile_rows(tile), :] = probs.astype(jnp.bfloat16)
                grad_scores = probs * (prob_grad_s[tile_rows(tile), :] - delta) * attn_scale
                grad_s[tile_rows(tile), :] = grad_scores.astype(jnp.bfloat16)
            at = pl.ds(key_at, tiles * tp)
            shape = (tiles * tp, plan.rows, HEAD_SIZE)
            dv_s[at, :, head_cols] += jnp.dot(prob_s[...], grads, preferred_element_type=jnp.float32).reshape(shape)
            dk_s[at, :, head_cols] += jnp.dot(grad_s[...], queries, preferred_element_type=jnp.float32).reshape(shape)
            query_sum = lax.dot_general(
                k_s[at, :, head_cols].reshape(tiles * block, HEAD_SIZE),
                grad_s[...],
                (((0,), (0,)), ((), ())),
                preferred_element_type=jnp.float32,
            )
            query_rows = query_sum.T.astype(jnp.bfloat16)
            for member in range(GROUP):
                dq_s[rows_at, :, pl.ds((head * GROUP + member) * HEAD_SIZE, HEAD_SIZE)] = query_rows[
                    member * block : (member + 1) * block
                ].reshape(tp, plan.rows, HEAD_SIZE)

        for head in range(heads):
            for copy in copies[head * loads // heads : (head + 1) * loads // heads]:
                copy.wait()
            for way in range(plan.ways):
                step(head, way)
            head_cols = pl.ds(head * HEAD_SIZE, HEAD_SIZE)
            for late, away in itertools.product((0, 1), (0, 1)):
                side = core + away * (cores - 1 - 2 * core)
                staged = part_s.at[late, away]
                for way, index in itertools.product(range(plan.ways), (0, 1)):
                    at = pl.ds(late * plan.pieces + (way * cores + side) * tp, tp)
                    total = (dk_s, dv_s)[index][at, :, head_cols]
                    staged[pl.ds(way * tp, tp), index, :, head_cols] = total.astype(jnp.bfloat16)
                if late or not away:
                    store(staged.at[:, :, :, head_cols], parts[2 * late + away].at[:, :, :, head_cols])
                else:
                    for piece in range(groups):
                        store(staged.at[piece, :, :, head_cols], before_far[piece].at[:, :, head_cols])
            done_part = pl.ds(head * query_width, query_width)
            for at, flip in enumerate(plan.flips):
                store(dq_s.at[group ^ flip, :, done_part], query_out[at].at[0, :, done_part])
        for copy in results:
            copy.wait()

    part = (groups, 2, plan.rows, key_cols)
    bf, fl = jnp.bfloat16, jnp.float32
    span = 2 * plan.pieces
    pairs = tiles * block * wide * heads * plan.ways
    out = pl.pallas_call(
        kernel,
        out_shape=[jax.ShapeDtypeStruct((1, plan.rows, query_cols), bf)] * groups
        + [jax.ShapeDtypeStruct(part, bf)] * 3
        + [jax.ShapeDtypeStruct(part[1:], bf)] * groups,
        in_specs=[SMEM] + [ANY] * (groups + 4 + len(after)),
        out_specs=[ANY] * (2 * groups + 3),
        scratch_shapes=[
            pltpu.VMEM((groups, plan.rows, query_cols), bf),
            pltpu.VMEM((groups, plan.rows, query_cols), bf),
            pltpu.VMEM((span, plan.rows, key_cols), bf),
            pltpu.VMEM((span, plan.rows, key_cols), bf),
            pltpu.VMEM((groups, plan.rows, query_cols), bf),
            pltpu.VMEM((span, plan.rows, key_cols), fl),
            pltpu.VMEM((span, plan.rows, key_cols), fl),
            pltpu.VMEM((2, 2) + part, bf),
            pltpu.VMEM((tiles * block, wide), fl),
            pltpu.VMEM((tiles * block, wide), fl),
            pltpu.VMEM((tiles * block, wide), bf),
            pltpu.VMEM((tiles * block, wide), bf),
            pltpu.SemaphoreType.DMA((loads,)),
            pltpu.SemaphoreType.DMA((stores,)),
        ],
        compiler_params=pltpu.CompilerParams(vmem_limit_bytes=VMEM_LIMIT),
        cost_estimate=pl.CostEstimate(flops=160 * pairs * HEAD_SIZE, bytes_accessed=6 << 20, transcendentals=pairs),
        name="backward",
    )(doc_lengths, *query_pieces, *key_arrays, *after)
    return out[:groups], out[groups : groups + 3], out[groups + 3 :]


def add_before(plan, mine, far, after):
    def kernel(mine_ref, *refs):
        for piece in range(plan.groups):
            total = mine_ref[piece].astype(jnp.float32) + refs[piece][...].astype(jnp.float32)
            refs[-1][piece] = total.astype(jnp.bfloat16)

    return pl.pallas_call(
        kernel,
        out_shape=jax.ShapeDtypeStruct(mine.shape, jnp.bfloat16),
        in_specs=[VMEM] * (1 + plan.groups) + [ANY] * len(after),
        out_specs=VMEM,
        cost_estimate=traffic(3 * mine.nbytes),
        name="add_before",
    )(mine, *far, *after)


def add_up(plan, mine, far, later, cost, riders):
    def kernel(mine_ref, far_ref, later_ref, *refs):
        _, _, group = plan.place()
        for at, flip in enumerate(plan.flips):
            piece, target = group ^ flip, refs[len(riders) + at]
            total = mine_ref[piece].astype(jnp.float32) + far_ref[piece].astype(jnp.float32)
            total = (total + later_ref[piece].astype(jnp.float32)).astype(jnp.bfloat16)
            if riders:
                target[0] = refs[at][0]
                target[1, :, : plan.key_cols] = total[0]
                target[1, :, plan.key_cols :] = total[1]
            else:
                target[...] = total

    shape = (2, plan.rows, 2 * plan.key_cols if riders else plan.key_cols)
    return pl.pallas_call(
        kernel,
        out_shape=[jax.ShapeDtypeStruct(shape, jnp.bfloat16)] * plan.groups,
        in_specs=[VMEM] * (3 + len(riders)),
        out_specs=[VMEM] * plan.groups,
        cost_estimate=traffic(cost),
        name="add_up",
    )(mine, far, later, *riders)


def join_columns(plan, sources, targets, width, name):
    flat = [piece for pieces in sources for piece in pieces]
    chunks = len(targets[0])
    chunk_width = width // chunks

    def kernel(*refs):
        pieces, outs, sem = refs[: len(flat)], refs[len(flat) : -1], refs[-1]
        _, _, group = plan.place()
        copies = []
        for out, parts in zip(outs, targets):
            for chunk, (which, row, column) in enumerate(parts):
                for at, flip in enumerate(plan.flips):
                    start = (group ^ flip) * width + chunk * chunk_width
                    copies.append(
                        pltpu.make_async_copy(
                            pieces[which * plan.groups + at].at[row, :, pl.ds(column, chunk_width)],
                            out.at[:, columns(start, chunk_width)],
                            sem.at[len(copies)],
                        )
                    )
        run_copies(copies)

    return pl.pallas_call(
        kernel,
        out_shape=[jax.ShapeDtypeStruct((plan.rows, width * plan.groups), jnp.bfloat16)] * len(targets),
        in_specs=[ANY] * len(flat),
        out_specs=[VMEM] * len(targets),
        scratch_shapes=[pltpu.SemaphoreType.DMA((len(targets) * chunks * plan.groups,))],
        cost_estimate=traffic(2 * sum(piece.nbytes for piece in flat)),
        name=name,
    )(*flat)


def per_device(queries, key_states, value_state_rows, out_grad, doc_lengths):
    plan = Plan(queries.shape[0])
    key_width = KEY_HEADS * HEAD_SIZE // plan.groups
    query_width = QUERY_HEADS * HEAD_SIZE // plan.groups

    def exchange(pieces):
        return [pieces[0]] + [plan.to_group(piece, flip) for piece, flip in zip(pieces[1:], plan.flips[1:])]

    key_parts = split_columns(plan, (key_states, value_state_rows), key_width, 1, "split_keys")[0]
    query_parts = split_columns(plan, (queries, out_grad), query_width, 1, "split_queries", after=(key_parts[0],))[0]
    pieces = exchange(key_parts)
    arrived = exchange(query_parts)
    own = gather_pieces(plan, pieces, HARD)
    before = gather_pieces(plan, [plan.to_slab(piece, 1) for piece in pieces], HARD, (own, *arrived[1:]))
    key_arrays = (own, plan.to_core(own), before, plan.to_core(before))
    after, wait = (), ()
    sums, query_outs, sent = [], [], []
    for chunk in range(plan.chunks):
        query_out, (before_mine, own_mine, own_far), before_far = backward(plan, chunk, doc_lengths, arrived, key_arrays, after)
        before_sum = add_before(plan, before_mine, [plan.to_core(piece) for piece in before_far], wait)
        later = plan.to_slab(before_sum, -1)
        sums.append((own_mine, plan.to_core(own_far), later))
        query_outs.append(query_out)
        if chunk < plan.chunks - 1 or plan.chunks == 1:
            sent.append(exchange(query_out))
            after = (before_sum, *sent[-1][1:])
        wait = (later,)
    query_from, key_from, value_from = ([(chunk, 0, 0) for chunk in range(len(sent))], [], [])
    for chunk in range(plan.chunks):
        last, first = chunk == plan.chunks - 1, chunk == 0
        riders = query_outs[-1] if first and not last else ()
        sent.append(exchange(add_up(plan, *sums[chunk], EASY if last else HARD, riders)))
        at = len(sent) - 1
        if riders:
            query_from.append((at, 0, 0))
        key_from.append((at, 1, 0) if riders else (at, 0, 0))
        value_from.append((at, 1, plan.key_cols) if riders else (at, 1, 0))
    (query_grad,) = join_columns(plan, sent[: plan.chunks], [query_from], query_width, "join_queries")
    key_gradient, value_gradient = join_columns(plan, sent, [key_from, value_from], key_width, "join_keys")
    return query_grad, key_gradient, value_gradient


def solution(mesh):
    split = P(("seq", "tp"), None)
    return jax.shard_map(
        per_device,
        mesh=mesh,
        in_specs=(split, split, split, split, P()),
        out_specs=(split, split, split),
        check_vma=False,
    )
```

```python
import itertools
import math

import jax
import jax.numpy as jnp
from jax import lax
from jax.experimental import pallas as pl
from jax.experimental.pallas import tpu as pltpu
from jax.sharding import PartitionSpec as P

QUERY_HEADS = 32
KEY_HEADS = 16
HEAD_SIZE = 128
WINDOW = 1024
GROUP = QUERY_HEADS // KEY_HEADS
AXES = ("seq", "tp")

attn_scale = 168.0 ** (-0.5)
masked_floor = -1e30

CHUNKS = 2
EASY, HARD = 1 << 21, 1 << 25
VMEM_LIMIT = 56 * 1024 * 1024
ANY = pl.BlockSpec(memory_space=pl.ANY)
VMEM = pl.BlockSpec(memory_space=pltpu.VMEM)
SMEM = pl.BlockSpec(memory_space=pltpu.SMEM)


class Plan:
    def __init__(self, rows):
        self.seq, self.tp = lax.axis_size("seq"), lax.axis_size("tp")
        self.rows = rows
        self.block = rows * self.tp
        self.slab = WINDOW // self.block
        self.cores = min(2, self.slab)
        self.ways = self.slab // self.cores
        self.groups = self.ways * self.tp
        self.key_heads = KEY_HEADS // self.groups
        self.chunks = min(CHUNKS, self.key_heads)
        self.heads = self.key_heads // self.chunks
        self.key_cols = self.heads * HEAD_SIZE
        self.query_cols = self.key_cols * GROUP
        self.pieces = self.slab * self.tp
        self.flips = sorted(range(self.groups), key=lambda flip: (flip > 0, -bin(flip).count("1")))

    def place(self):
        seq, tp = lax.axis_index("seq"), lax.axis_index("tp")
        inner = lax.rem(seq, self.slab)
        core = lax.rem(inner, self.cores)
        return seq - inner, core, (inner // self.cores) * self.tp + tp

    def routes(self, move):
        pairs = []
        for seq in range(self.seq):
            for tp in range(self.tp):
                slab, inner = divmod(seq, self.slab)
                way, core = divmod(inner, self.cores)
                to_slab, to_core, to_group = move(slab, core, way * self.tp + tp)
                to_slab %= self.seq // self.slab
                target = (to_slab * self.slab + to_group // self.tp * self.cores + to_core) * self.tp + to_group % self.tp
                pairs.append((seq * self.tp + tp, target))
        return pairs

    def to_group(self, value, flip):
        return lax.ppermute(value, AXES, self.routes(lambda slab, core, group: (slab, core, group ^ flip)))

    def to_core(self, value):
        return lax.ppermute(value, AXES, self.routes(lambda slab, core, group: (slab, self.cores - 1 - core, group)))

    def to_slab(self, value, step):
        return lax.ppermute(value, AXES, self.routes(lambda slab, core, group: (slab + step, core, group)))


def run_copies(copies):
    for copy in copies:
        copy.start()
    for copy in copies:
        copy.wait()


def traffic(count):
    return pl.CostEstimate(flops=0, bytes_accessed=count, transcendentals=0)


def columns(start, width):
    return pl.ds(pl.multiple_of(start, HEAD_SIZE), width)


def split_columns(plan, arrays, width, chunks, name, after=()):
    chunk_width = width // chunks

    def kernel(*refs):
        sources, targets, sem = refs[: len(arrays)], refs[len(arrays) + len(after) : -1], refs[-1]
        _, _, group = plan.place()
        copies = []
        for chunk in range(chunks):
            for at, flip in enumerate(plan.flips):
                start = (group ^ flip) * width + chunk * chunk_width
                for index, source in enumerate(sources):
                    copies.append(
                        pltpu.make_async_copy(
                            source.at[:, columns(start, chunk_width)],
                            targets[chunk * plan.groups + at].at[index],
                            sem.at[len(copies)],
                        )
                    )
        run_copies(copies)

    count = chunks * plan.groups
    shape = jax.ShapeDtypeStruct((len(arrays), plan.rows, chunk_width), jnp.bfloat16)
    out = pl.pallas_call(
        kernel,
        out_shape=[shape] * count,
        in_specs=[ANY] * (len(arrays) + len(after)),
        out_specs=[VMEM] * count,
        scratch_shapes=[pltpu.SemaphoreType.DMA((count * len(arrays),))],
        cost_estimate=traffic(2 * sum(array.nbytes for array in arrays)),
        name=name,
    )(*arrays, *after)
    return [out[chunk * plan.groups : (chunk + 1) * plan.groups] for chunk in range(chunks)]


def ordered(value, cost, after):
    def kernel(*refs):
        pass

    return pl.pallas_call(
        kernel,
        out_shape=jax.ShapeDtypeStruct(value.shape, value.dtype),
        in_specs=[ANY] * (1 + len(after)),
        out_specs=ANY,
        input_output_aliases={0: 0},
        cost_estimate=traffic(cost),
        name="ordered",
    )(value, *after)


def backward(plan, chunk, doc_lengths, query_pieces, key_arrays, after):
    tiles = plan.slab + 1
    block, groups, tp, cores = plan.block, plan.groups, plan.tp, plan.cores
    heads, key_cols, query_cols = plan.heads, plan.key_cols, plan.query_cols
    wide = GROUP * block
    query_width = HEAD_SIZE * GROUP
    exponent_scale = attn_scale * math.log2(math.e)
    loads = heads * 5 * groups
    stores = heads * (2 * groups + 3)

    def kernel(docs, *refs):
        pieces, refs = refs[:groups], refs[groups:]
        key_refs, refs = refs[:4], refs[4:]
        refs = refs[len(after) :]
        query_out, refs = refs[:groups], refs[groups:]
        before_mine, own_mine, own_far, refs = *refs[:3], refs[3:]
        parts = (before_mine, None, own_mine, own_far)
        before_far, refs = refs[:groups], refs[groups:]
        qo_s, kv_s, dq_s, dk_s, dv_s, part_s, score_s, prob_grad_s, prob_s, grad_s, sem, out_sem = refs
        q_s, o_s, k_s, v_s = qo_s.at[0], qo_s.at[1], kv_s.at[0], kv_s.at[1]
        slab_seq, core, group = plan.place()

        copies, results = [], []

        def block_of(late, away, flip):
            side = core + away * (cores - 1 - 2 * core)
            return late * plan.pieces + ((group ^ flip) // tp * cores + side) * tp + lax.rem(group ^ flip, tp)

        def load(source, target):
            copies.append(pltpu.make_async_copy(source, target, sem.at[len(copies)]))
            copies[-1].start()

        def store(source, target):
            results.append(pltpu.make_async_copy(source, target, out_sem.at[len(results)]))
            results[-1].start()

        for head in range(heads):
            here, there = pl.ds(head * query_width, query_width), pl.ds((chunk * heads + head) * query_width, query_width)
            for flip, piece in zip(plan.flips, pieces):
                load(piece.at[:, :, there], qo_s.at[:, group ^ flip, :, here])
            here, there = pl.ds(head * HEAD_SIZE, HEAD_SIZE), pl.ds((chunk * heads + head) * HEAD_SIZE, HEAD_SIZE)
            for source, (late, away) in zip(key_refs, itertools.product((1, 0), (0, 1))):
                for at, flip in enumerate(plan.flips):
                    load(source.at[at, :, :, there], kv_s.at[:, block_of(late, away, flip), :, here])
        dk_s[...] = jnp.zeros_like(dk_s)
        dv_s[...] = jnp.zeros_like(dv_s)

        def step(head, way):
            key_at = (way * cores + core) * tp
            head_cols = pl.ds(head * HEAD_SIZE, HEAD_SIZE)
            rows_at = pl.ds(way * tp, tp)

            def both(ref):
                parts = [
                    ref[rows_at, :, pl.ds((head * GROUP + member) * HEAD_SIZE, HEAD_SIZE)].reshape(block, HEAD_SIZE)
                    for member in range(GROUP)
                ]
                return jnp.concatenate(parts, axis=0)

            queries, grads = both(q_s), both(o_s)
            inner = lax.broadcasted_iota(jnp.int32, (1, block), 1)
            inner = jnp.concatenate([inner] * GROUP, axis=1)
            first = (slab_seq + way * cores + core) * block
            position = inner + first
            lowest = position - (WINDOW - 1)
            start = jnp.int32(0)
            for doc in range(docs.shape[0]):
                lowest = jnp.where(position >= start, jnp.maximum(lowest, start), lowest)
                start = start + docs[doc]
            lowest = lowest - (first - WINDOW)

            def key_rows(ref, tile):
                return ref[pl.ds(key_at + tile * tp, tp), :, head_cols].reshape(block, HEAD_SIZE)

            def tile_rows(tile):
                return pl.ds(tile * block, block)

            peak = jnp.full((1, wide), masked_floor, jnp.float32)
            for tile in range(tiles):
                scores = lax.dot_general(
                    key_rows(k_s, tile), queries, (((1,), (1,)), ((), ())), preferred_element_type=jnp.float32
                )
                row = lax.broadcasted_iota(jnp.int32, (block, wide), 0)
                allowed = row >= lowest - tile * block
                if tile == tiles - 1:
                    allowed = allowed & (row <= inner)
                scores = jnp.where(allowed, scores, masked_floor)
                peak = jnp.maximum(peak, jnp.max(scores, axis=0, keepdims=True))
                score_s[tile_rows(tile), :] = scores
            peak = peak * exponent_scale
            total = jnp.zeros((1, wide), jnp.float32)
            delta = jnp.zeros((1, wide), jnp.float32)
            for tile in range(tiles):
                raised = jnp.exp2(score_s[tile_rows(tile), :] * exponent_scale - peak)
                prob_grad = lax.dot_general(
                    key_rows(v_s, tile), grads, (((1,), (1,)), ((), ())), preferred_element_type=jnp.float32
                )
                total = total + jnp.sum(raised, axis=0, keepdims=True)
                delta = delta + jnp.sum(raised * prob_grad, axis=0, keepdims=True)
                score_s[tile_rows(tile), :] = raised
                prob_grad_s[tile_rows(tile), :] = prob_grad
            inverse = 1.0 / total
            delta = delta * inverse
            for tile in range(tiles):
                probs = score_s[tile_rows(tile), :] * inverse
                prob_s[tile_rows(tile), :] = probs.astype(jnp.bfloat16)
                grad_scores = probs * (prob_grad_s[tile_rows(tile), :] - delta) * attn_scale
                grad_s[tile_rows(tile), :] = grad_scores.astype(jnp.bfloat16)
            at = pl.ds(key_at, tiles * tp)
            shape = (tiles * tp, plan.rows, HEAD_SIZE)
            dv_s[at, :, head_cols] += jnp.dot(prob_s[...], grads, preferred_element_type=jnp.float32).reshape(shape)
            dk_s[at, :, head_cols] += jnp.dot(grad_s[...], queries, preferred_element_type=jnp.float32).reshape(shape)
            query_sum = lax.dot_general(
                k_s[at, :, head_cols].reshape(tiles * block, HEAD_SIZE),
                grad_s[...],
                (((0,), (0,)), ((), ())),
                preferred_element_type=jnp.float32,
            )
            query_rows = query_sum.T.astype(jnp.bfloat16)
            for member in range(GROUP):
                dq_s[rows_at, :, pl.ds((head * GROUP + member) * HEAD_SIZE, HEAD_SIZE)] = query_rows[
                    member * block : (member + 1) * block
                ].reshape(tp, plan.rows, HEAD_SIZE)

        for head in range(heads):
            for copy in copies[head * loads // heads : (head + 1) * loads // heads]:
                copy.wait()
            for way in range(plan.ways):
                step(head, way)
            head_cols = pl.ds(head * HEAD_SIZE, HEAD_SIZE)
            for late, away in itertools.product((0, 1), (0, 1)):
                staged = part_s.at[late, away]
                for (at, flip), index in itertools.product(enumerate(plan.flips), (0, 1)):
                    total = (dk_s, dv_s)[index][block_of(late, away, flip), :, head_cols]
                    staged[at, index, :, head_cols] = total.astype(jnp.bfloat16)
                if late or not away:
                    store(staged.at[:, :, :, head_cols], parts[2 * late + away].at[:, :, :, head_cols])
                else:
                    for piece in range(groups):
                        store(staged.at[piece, :, :, head_cols], before_far[piece].at[:, :, head_cols])
            done_part = pl.ds(head * query_width, query_width)
            for at, flip in enumerate(plan.flips):
                store(dq_s.at[group ^ flip, :, done_part], query_out[at].at[0, :, done_part])
        for copy in results:
            copy.wait()

    part = (groups, 2, plan.rows, key_cols)
    bf, fl = jnp.bfloat16, jnp.float32
    span = 2 * plan.pieces
    pairs = tiles * block * wide * heads * plan.ways
    out = pl.pallas_call(
        kernel,
        out_shape=[jax.ShapeDtypeStruct((1, plan.rows, query_cols), bf)] * groups
        + [jax.ShapeDtypeStruct(part, bf)] * 3
        + [jax.ShapeDtypeStruct(part[1:], bf)] * groups,
        in_specs=[SMEM] + [ANY] * (groups + 4 + len(after)),
        out_specs=[ANY] * (2 * groups + 3),
        scratch_shapes=[
            pltpu.VMEM((2, groups, plan.rows, query_cols), bf),
            pltpu.VMEM((2, span, plan.rows, key_cols), bf),
            pltpu.VMEM((groups, plan.rows, query_cols), bf),
            pltpu.VMEM((span, plan.rows, key_cols), fl),
            pltpu.VMEM((span, plan.rows, key_cols), fl),
            pltpu.VMEM((2, 2) + part, bf),
            pltpu.VMEM((tiles * block, wide), fl),
            pltpu.VMEM((tiles * block, wide), fl),
            pltpu.VMEM((tiles * block, wide), bf),
            pltpu.VMEM((tiles * block, wide), bf),
            pltpu.SemaphoreType.DMA((loads,)),
            pltpu.SemaphoreType.DMA((stores,)),
        ],
        compiler_params=pltpu.CompilerParams(vmem_limit_bytes=VMEM_LIMIT),
        cost_estimate=pl.CostEstimate(flops=160 * pairs * HEAD_SIZE, bytes_accessed=6 << 20, transcendentals=pairs),
        name="backward",
    )(doc_lengths, *query_pieces, *key_arrays, *after)
    return out[:groups], out[groups : groups + 3], out[groups + 3 :]


def add_up(*parts):
    total = parts[0].astype(jnp.float32)
    for part in parts[1:]:
        total = total + part.astype(jnp.float32)
    return total.astype(jnp.bfloat16)


def join_columns(plan, sources, targets, width, name):
    flat = [piece for pieces in sources for piece in pieces]
    chunks = len(targets[0])
    chunk_width = width // chunks

    def kernel(*refs):
        pieces, outs, sem = refs[: len(flat)], refs[len(flat) : -1], refs[-1]
        _, _, group = plan.place()
        copies = []
        for out, parts in zip(outs, targets):
            for chunk, (which, row, column) in enumerate(parts):
                for at, flip in enumerate(plan.flips):
                    start = (group ^ flip) * width + chunk * chunk_width
                    copies.append(
                        pltpu.make_async_copy(
                            pieces[which * plan.groups + at].at[row, :, pl.ds(column, chunk_width)],
                            out.at[:, columns(start, chunk_width)],
                            sem.at[len(copies)],
                        )
                    )
        run_copies(copies)

    return pl.pallas_call(
        kernel,
        out_shape=[jax.ShapeDtypeStruct((plan.rows, width * plan.groups), jnp.bfloat16)] * len(targets),
        in_specs=[ANY] * len(flat),
        out_specs=[VMEM] * len(targets),
        scratch_shapes=[pltpu.SemaphoreType.DMA((len(targets) * chunks * plan.groups,))],
        cost_estimate=traffic(2 * sum(piece.nbytes for piece in flat)),
        name=name,
    )(*flat)


def per_device(queries, key_states, value_state_rows, out_grad, doc_lengths):
    plan = Plan(queries.shape[0])
    key_width = KEY_HEADS * HEAD_SIZE // plan.groups
    query_width = QUERY_HEADS * HEAD_SIZE // plan.groups

    def exchange(pieces):
        return [pieces[0]] + [plan.to_group(piece, flip) for piece, flip in zip(pieces[1:], plan.flips[1:])]

    key_parts = split_columns(plan, (key_states, value_state_rows), key_width, 1, "split_keys")[0]
    query_parts = split_columns(plan, (queries, out_grad), query_width, 1, "split_queries", after=(key_parts[0],))[0]
    pieces = exchange(key_parts)
    arrived = exchange(query_parts)
    own_first = ordered(pieces[0], HARD, pieces[1:])
    own = jnp.stack([own_first, *pieces[1:]])
    own_other = plan.to_core(own)
    moved = [plan.to_slab(pieces[0], 1), plan.to_slab(pieces[1], 1)]
    if plan.groups > 2:
        rest = plan.to_slab(jnp.stack(pieces[2:]), 1)
        moved = moved + [rest[at] for at in range(plan.groups - 2)]
    before = jnp.stack([ordered(moved[0], HARD, (own_first, *arrived[1:])), *moved[1:]])
    before_other = plan.to_core(before)
    key_arrays = (own, own_other, before, before_other)
    after, hold = (), ()
    sums, query_outs, sent = [], [], []
    for chunk in range(plan.chunks):
        query_out, (before_mine, own_mine, own_far), before_far = backward(plan, chunk, doc_lengths, arrived, key_arrays, after)
        if hold:
            before_mine = ordered(before_mine, EASY, hold)
        before_sum = add_up(before_mine, jnp.stack([plan.to_core(piece) for piece in before_far]))
        later = plan.to_slab(before_sum, -1)
        sums.append((own_mine, plan.to_core(own_far), later))
        query_outs.append(query_out)
        if chunk < plan.chunks - 1 or plan.chunks == 1:
            sent.append(exchange(query_out))
            after = (before_sum, *sent[-1][1:])
        hold = (later,)
    query_from, key_from, value_from = ([(chunk, 0, 0) for chunk in range(len(sent))], [], [])
    for chunk in range(plan.chunks):
        own_mine, own_far, later = sums[chunk]
        riders = chunk == 0 and plan.chunks > 1
        if riders:
            own_mine = ordered(own_mine, HARD, query_outs[-1][:1])
        messages = [add_up(own_mine[at], own_far[at], later[at]) for at in range(plan.groups)]
        if riders:
            messages = [
                jnp.concatenate([rider, jnp.concatenate([message[0], message[1]], axis=1)[None]])
                for rider, message in zip(query_outs[-1], messages)
            ]
            query_from.append((len(sent), 0, 0))
        sent.append(exchange(messages))
        at = len(sent) - 1
        key_from.append((at, 1, 0) if riders else (at, 0, 0))
        value_from.append((at, 1, plan.key_cols) if riders else (at, 1, 0))
    (query_grad,) = join_columns(plan, sent[: plan.chunks], [query_from], query_width, "join_queries")
    key_gradient, value_gradient = join_columns(plan, sent, [key_from, value_from], key_width, "join_keys")
    return query_grad, key_gradient, value_gradient


def solution(mesh):
    split = P(("seq", "tp"), None)
    return jax.shard_map(
        per_device,
        mesh=mesh,
        in_specs=(split, split, split, split, P()),
        out_specs=(split, split, split),
        check_vma=False,
    )
```

```python
import itertools
import math

import jax
import jax.numpy as jnp
from jax import lax
from jax.experimental import pallas as pl
from jax.experimental.pallas import tpu as pltpu
from jax.sharding import PartitionSpec as P

QUERY_HEADS = 32
KEY_HEADS = 16
HEAD_SIZE = 128
WINDOW = 1024
GROUP = QUERY_HEADS // KEY_HEADS
AXES = ("seq", "tp")

attn_scale = 168.0 ** (-0.5)
masked_floor = -1e30

CHUNKS = 2
EASY, HARD = 1 << 21, 1 << 25
VMEM_LIMIT = 56 * 1024 * 1024
ANY = pl.BlockSpec(memory_space=pl.ANY)
VMEM = pl.BlockSpec(memory_space=pltpu.VMEM)
SMEM = pl.BlockSpec(memory_space=pltpu.SMEM)


class Plan:
    def __init__(self, rows):
        self.seq, self.tp = lax.axis_size("seq"), lax.axis_size("tp")
        self.rows = rows
        self.block = rows * self.tp
        self.slab = WINDOW // self.block
        self.cores = min(2, self.slab)
        self.ways = self.slab // self.cores
        self.groups = self.ways * self.tp
        self.key_heads = KEY_HEADS // self.groups
        self.chunks = min(CHUNKS, self.key_heads)
        self.heads = self.key_heads // self.chunks
        self.key_cols = self.heads * HEAD_SIZE
        self.query_cols = self.key_cols * GROUP
        self.pieces = self.slab * self.tp
        self.flips = sorted(range(self.groups), key=lambda flip: (flip > 0, -bin(flip).count("1")))

    def place(self):
        seq, tp = lax.axis_index("seq"), lax.axis_index("tp")
        inner = lax.rem(seq, self.slab)
        core = lax.rem(inner, self.cores)
        return seq - inner, core, (inner // self.cores) * self.tp + tp

    def routes(self, move):
        pairs = []
        for seq in range(self.seq):
            for tp in range(self.tp):
                slab, inner = divmod(seq, self.slab)
                way, core = divmod(inner, self.cores)
                to_slab, to_core, to_group = move(slab, core, way * self.tp + tp)
                to_slab %= self.seq // self.slab
                target = (to_slab * self.slab + to_group // self.tp * self.cores + to_core) * self.tp + to_group % self.tp
                pairs.append((seq * self.tp + tp, target))
        return pairs

    def to_group(self, value, flip):
        return lax.ppermute(value, AXES, self.routes(lambda slab, core, group: (slab, core, group ^ flip)))

    def to_core(self, value):
        return lax.ppermute(value, AXES, self.routes(lambda slab, core, group: (slab, self.cores - 1 - core, group)))

    def to_slab(self, value, step):
        return lax.ppermute(value, AXES, self.routes(lambda slab, core, group: (slab + step, core, group)))


def run_copies(copies):
    for copy in copies:
        copy.start()
    for copy in copies:
        copy.wait()


def traffic(count):
    return pl.CostEstimate(flops=0, bytes_accessed=count, transcendentals=0)


def columns(start, width):
    return pl.ds(pl.multiple_of(start, HEAD_SIZE), width)


def split_columns(plan, arrays, width, chunks, name, after=()):
    chunk_width = width // chunks

    def kernel(*refs):
        sources, targets, sem = refs[: len(arrays)], refs[len(arrays) + len(after) : -1], refs[-1]
        _, _, group = plan.place()
        copies = []
        for chunk in range(chunks):
            for at, flip in enumerate(plan.flips):
                start = (group ^ flip) * width + chunk * chunk_width
                for index, source in enumerate(sources):
                    copies.append(
                        pltpu.make_async_copy(
                            source.at[:, columns(start, chunk_width)],
                            targets[chunk * plan.groups + at].at[index],
                            sem.at[len(copies)],
                        )
                    )
        run_copies(copies)

    count = chunks * plan.groups
    shape = jax.ShapeDtypeStruct((len(arrays), plan.rows, chunk_width), jnp.bfloat16)
    out = pl.pallas_call(
        kernel,
        out_shape=[shape] * count,
        in_specs=[ANY] * (len(arrays) + len(after)),
        out_specs=[VMEM] * count,
        scratch_shapes=[pltpu.SemaphoreType.DMA((count * len(arrays),))],
        cost_estimate=traffic(2 * sum(array.nbytes for array in arrays)),
        name=name,
    )(*arrays, *after)
    return [out[chunk * plan.groups : (chunk + 1) * plan.groups] for chunk in range(chunks)]


def ordered(value, cost, after):
    def kernel(*refs):
        pass

    return pl.pallas_call(
        kernel,
        out_shape=jax.ShapeDtypeStruct(value.shape, value.dtype),
        in_specs=[ANY] * (1 + len(after)),
        out_specs=ANY,
        input_output_aliases={0: 0},
        cost_estimate=traffic(cost),
        name="ordered",
    )(value, *after)


def backward(plan, chunk, doc_lengths, query_pieces, key_arrays, earlier, after):
    tiles = plan.slab + 1
    block, groups, tp, cores = plan.block, plan.groups, plan.tp, plan.cores
    heads, key_cols, query_cols = plan.heads, plan.key_cols, plan.query_cols
    wide = GROUP * block
    query_width = HEAD_SIZE * GROUP
    exponent_scale = attn_scale * math.log2(math.e)
    loads = heads * 5 * groups
    stores = heads * (2 * groups + 3) + len(earlier)

    def kernel(docs, *refs):
        pieces, refs = refs[:groups], refs[groups:]
        key_refs, refs = refs[:4], refs[4:]
        early, refs = refs[: len(earlier)], refs[len(earlier) + len(after) :]
        query_out, refs = refs[:groups], refs[groups:]
        before_mine, own_mine, own_far, refs = *refs[:3], refs[3:]
        parts = (before_mine, None, own_mine, own_far)
        before_far, refs = refs[:groups], refs[groups:]
        qo_s, kv_s, dq_s, early_s, dk_s, dv_s, part_s, score_s, prob_grad_s, prob_s, grad_s, sem, out_sem = refs
        q_s, o_s, k_s, v_s = qo_s.at[0], qo_s.at[1], kv_s.at[0], kv_s.at[1]
        slab_seq, core, group = plan.place()

        copies, results = [], []

        def block_of(late, away, flip):
            side = core + away * (cores - 1 - 2 * core)
            return late * plan.pieces + ((group ^ flip) // tp * cores + side) * tp + lax.rem(group ^ flip, tp)

        def load(source, target):
            copies.append(pltpu.make_async_copy(source, target, sem.at[len(copies)]))
            copies[-1].start()

        def store(source, target):
            results.append(pltpu.make_async_copy(source, target, out_sem.at[len(results)]))
            results[-1].start()

        for head in range(heads):
            here, there = pl.ds(head * query_width, query_width), pl.ds((chunk * heads + head) * query_width, query_width)
            for flip, piece in zip(plan.flips, pieces):
                load(piece.at[:, :, there], qo_s.at[:, group ^ flip, :, here])
            here, there = pl.ds(head * HEAD_SIZE, HEAD_SIZE), pl.ds((chunk * heads + head) * HEAD_SIZE, HEAD_SIZE)
            for source, (late, away) in zip(key_refs, itertools.product((1, 0), (0, 1))):
                for at, flip in enumerate(plan.flips):
                    load(source.at[at, :, :, there], kv_s.at[:, block_of(late, away, flip), :, here])
        for at, source in enumerate(early):
            load(source, early_s.at[at])
        dk_s[...] = jnp.zeros_like(dk_s)
        dv_s[...] = jnp.zeros_like(dv_s)

        def step(head, way):
            key_at = (way * cores + core) * tp
            head_cols = pl.ds(head * HEAD_SIZE, HEAD_SIZE)
            rows_at = pl.ds(way * tp, tp)

            def both(ref):
                parts = [
                    ref[rows_at, :, pl.ds((head * GROUP + member) * HEAD_SIZE, HEAD_SIZE)].reshape(block, HEAD_SIZE)
                    for member in range(GROUP)
                ]
                return jnp.concatenate(parts, axis=0)

            queries, grads = both(q_s), both(o_s)
            inner = lax.broadcasted_iota(jnp.int32, (1, block), 1)
            inner = jnp.concatenate([inner] * GROUP, axis=1)
            first = (slab_seq + way * cores + core) * block
            position = inner + first
            lowest = position - (WINDOW - 1)
            start = jnp.int32(0)
            for doc in range(docs.shape[0]):
                lowest = jnp.where(position >= start, jnp.maximum(lowest, start), lowest)
                start = start + docs[doc]
            lowest = lowest - (first - WINDOW)

            def key_rows(ref, tile):
                return ref[pl.ds(key_at + tile * tp, tp), :, head_cols].reshape(block, HEAD_SIZE)

            def tile_rows(tile):
                return pl.ds(tile * block, block)

            peak = jnp.full((1, wide), masked_floor, jnp.float32)
            for tile in range(tiles):
                scores = lax.dot_general(
                    key_rows(k_s, tile), queries, (((1,), (1,)), ((), ())), preferred_element_type=jnp.float32
                )
                row = lax.broadcasted_iota(jnp.int32, (block, wide), 0)
                allowed = row >= lowest - tile * block
                if tile == tiles - 1:
                    allowed = allowed & (row <= inner)
                scores = jnp.where(allowed, scores, masked_floor)
                peak = jnp.maximum(peak, jnp.max(scores, axis=0, keepdims=True))
                score_s[tile_rows(tile), :] = scores
            peak = peak * exponent_scale
            total = jnp.zeros((1, wide), jnp.float32)
            delta = jnp.zeros((1, wide), jnp.float32)
            for tile in range(tiles):
                raised = jnp.exp2(score_s[tile_rows(tile), :] * exponent_scale - peak)
                prob_grad = lax.dot_general(
                    key_rows(v_s, tile), grads, (((1,), (1,)), ((), ())), preferred_element_type=jnp.float32
                )
                total = total + jnp.sum(raised, axis=0, keepdims=True)
                delta = delta + jnp.sum(raised * prob_grad, axis=0, keepdims=True)
                score_s[tile_rows(tile), :] = raised
                prob_grad_s[tile_rows(tile), :] = prob_grad
            inverse = 1.0 / total
            delta = delta * inverse
            for tile in range(tiles):
                probs = score_s[tile_rows(tile), :] * inverse
                prob_s[tile_rows(tile), :] = probs.astype(jnp.bfloat16)
                grad_scores = probs * (prob_grad_s[tile_rows(tile), :] - delta) * attn_scale
                grad_s[tile_rows(tile), :] = grad_scores.astype(jnp.bfloat16)
            at = pl.ds(key_at, tiles * tp)
            shape = (tiles * tp, plan.rows, HEAD_SIZE)
            dv_s[at, :, head_cols] += jnp.dot(prob_s[...], grads, preferred_element_type=jnp.float32).reshape(shape)
            dk_s[at, :, head_cols] += jnp.dot(grad_s[...], queries, preferred_element_type=jnp.float32).reshape(shape)
            query_sum = lax.dot_general(
                k_s[at, :, head_cols].reshape(tiles * block, HEAD_SIZE),
                grad_s[...],
                (((0,), (0,)), ((), ())),
                preferred_element_type=jnp.float32,
            )
            query_rows = query_sum.T.astype(jnp.bfloat16)
            for member in range(GROUP):
                dq_s[rows_at, :, pl.ds((head * GROUP + member) * HEAD_SIZE, HEAD_SIZE)] = query_rows[
                    member * block : (member + 1) * block
                ].reshape(tp, plan.rows, HEAD_SIZE)

        for head in range(heads):
            for copy in copies[head * loads // heads : (head + 1) * loads // heads]:
                copy.wait()
            for way in range(plan.ways):
                step(head, way)
            if head == 0:
                for copy in copies[loads:]:
                    copy.wait()
                for at, target in enumerate(query_out[: len(early)]):
                    store(early_s.at[at], target.at[pl.ds(0, chunk)])
            head_cols = pl.ds(head * HEAD_SIZE, HEAD_SIZE)
            for late, away in itertools.product((0, 1), (0, 1)):
                staged = part_s.at[late, away]
                for (at, flip), index in itertools.product(enumerate(plan.flips), (0, 1)):
                    total = (dk_s, dv_s)[index][block_of(late, away, flip), :, head_cols]
                    staged[at, index, :, head_cols] = total.astype(jnp.bfloat16)
                if late or not away:
                    store(staged.at[:, :, :, head_cols], parts[2 * late + away].at[:, :, :, head_cols])
                else:
                    for piece in range(groups):
                        store(staged.at[piece, :, :, head_cols], before_far[piece].at[:, :, head_cols])
            done_part = pl.ds(head * query_width, query_width)
            for at, flip in enumerate(plan.flips):
                store(dq_s.at[group ^ flip, :, done_part], query_out[at].at[chunk, :, done_part])
        for copy in results:
            copy.wait()

    part = (groups, 2, plan.rows, key_cols)
    bf, fl = jnp.bfloat16, jnp.float32
    span = 2 * plan.pieces
    pairs = tiles * block * wide * heads * plan.ways
    out = pl.pallas_call(
        kernel,
        out_shape=[jax.ShapeDtypeStruct((chunk + 1, plan.rows, query_cols), bf)] * groups
        + [jax.ShapeDtypeStruct(part, bf)] * 3
        + [jax.ShapeDtypeStruct(part[1:], bf)] * groups,
        in_specs=[SMEM] + [ANY] * (groups + 4 + len(earlier) + len(after)),
        out_specs=[ANY] * (2 * groups + 3),
        scratch_shapes=[
            pltpu.VMEM((2, groups, plan.rows, query_cols), bf),
            pltpu.VMEM((2, span, plan.rows, key_cols), bf),
            pltpu.VMEM((groups, plan.rows, query_cols), bf),
            pltpu.VMEM((groups, max(chunk, 1), plan.rows, query_cols), bf),
            pltpu.VMEM((span, plan.rows, key_cols), fl),
            pltpu.VMEM((span, plan.rows, key_cols), fl),
            pltpu.VMEM((2, 2) + part, bf),
            pltpu.VMEM((tiles * block, wide), fl),
            pltpu.VMEM((tiles * block, wide), fl),
            pltpu.VMEM((tiles * block, wide), bf),
            pltpu.VMEM((tiles * block, wide), bf),
            pltpu.SemaphoreType.DMA((loads + len(earlier),)),
            pltpu.SemaphoreType.DMA((stores,)),
        ],
        compiler_params=pltpu.CompilerParams(vmem_limit_bytes=VMEM_LIMIT),
        cost_estimate=pl.CostEstimate(flops=160 * pairs * HEAD_SIZE, bytes_accessed=6 << 20, transcendentals=pairs),
        name="backward",
    )(doc_lengths, *query_pieces, *key_arrays, *earlier, *after)
    return out[:groups], out[groups : groups + 3], out[groups + 3 :]


def token(arrays):
    return sum(array.reshape(-1, array.shape[-1])[:16, :HEAD_SIZE] for array in arrays)


def add_up(*parts):
    total = parts[0].astype(jnp.float32)
    for part in parts[1:]:
        total = total + part.astype(jnp.float32)
    return total.astype(jnp.bfloat16)


def join_columns(plan, sources, targets, width, name):
    flat = [piece for pieces in sources for piece in pieces[::-1]]
    chunks = len(targets[0])
    chunk_width = width // chunks

    def kernel(*refs):
        pieces, outs, sem = refs[: len(flat)], refs[len(flat) : -1], refs[-1]
        _, _, group = plan.place()
        copies = []
        for out, parts in zip(outs, targets):
            for chunk, (which, row, column) in enumerate(parts):
                for at, flip in enumerate(plan.flips):
                    start = (group ^ flip) * width + chunk * chunk_width
                    copies.append(
                        pltpu.make_async_copy(
                            pieces[(which + 1) * plan.groups - 1 - at].at[row, :, pl.ds(column, chunk_width)],
                            out.at[:, columns(start, chunk_width)],
                            sem.at[len(copies)],
                        )
                    )
        run_copies(copies)

    return pl.pallas_call(
        kernel,
        out_shape=[jax.ShapeDtypeStruct((plan.rows, width * plan.groups), jnp.bfloat16)] * len(targets),
        in_specs=[ANY] * len(flat),
        out_specs=[VMEM] * len(targets),
        scratch_shapes=[pltpu.SemaphoreType.DMA((len(targets) * chunks * plan.groups,))],
        cost_estimate=traffic(2 * sum(piece.nbytes for piece in flat)),
        name=name,
    )(*flat)


def per_device(queries, key_states, value_state_rows, out_grad, doc_lengths):
    plan = Plan(queries.shape[0])
    key_width = KEY_HEADS * HEAD_SIZE // plan.groups
    query_width = QUERY_HEADS * HEAD_SIZE // plan.groups

    def exchange(pieces):
        return [pieces[0]] + [plan.to_group(piece, flip) for piece, flip in zip(pieces[1:], plan.flips[1:])]

    key_parts = split_columns(plan, (key_states, value_state_rows), key_width, 1, "split_keys")[0]
    query_parts = split_columns(plan, (queries, out_grad), query_width, 1, "split_queries", after=(key_parts[0],))[0]
    pieces = exchange(key_parts)
    arrived = exchange(query_parts)
    own_first = ordered(pieces[0], HARD, pieces[1:])
    own = jnp.stack([own_first, *pieces[1:]])
    own_other = plan.to_core(own)
    moved = [plan.to_slab(pieces[0], 1), plan.to_slab(pieces[1], 1)]
    if plan.groups > 2:
        rest = plan.to_slab(jnp.stack(pieces[2:]), 1)
        moved = moved + [rest[at] for at in range(plan.groups - 2)]
    before = jnp.stack([ordered(moved[0], HARD, (own_first, *arrived[1:])), *moved[1:]])
    before_other = plan.to_core(before)
    key_arrays = (own, own_other, before, before_other)
    after, hold, query_out = (), (), ()
    sums = []
    for chunk in range(plan.chunks):
        query_out, (before_mine, own_mine, own_far), before_far = backward(
            plan, chunk, doc_lengths, arrived, key_arrays, query_out, after
        )
        if hold:
            before_mine = ordered(before_mine, EASY, hold)
        before_sum = add_up(before_mine, jnp.stack([plan.to_core(piece) for piece in before_far]))
        later = plan.to_slab(before_sum, -1)
        sums.append((own_mine, plan.to_core(own_far), later))
        after, hold = (token((before_sum,)),), (later,)
    query_sent = exchange(query_out)
    key_sent = []
    for chunk, (own_mine, own_far, later) in enumerate(sums):
        if chunk < plan.chunks - 1:
            own_mine = ordered(own_mine, HARD, query_out[:1])
        key_sent.append(exchange([add_up(own_mine[at], own_far[at], later[at]) for at in range(plan.groups)]))
    chunks = range(plan.chunks)
    (query_grad,) = join_columns(plan, [query_sent], [[(0, chunk, 0) for chunk in chunks]], query_width, "join_queries")
    key_gradient, value_gradient = join_columns(
        plan, key_sent, [[(chunk, index, 0) for chunk in chunks] for index in (0, 1)], key_width, "join_keys"
    )
    return query_grad, key_gradient, value_gradient


def solution(mesh):
    split = P(("seq", "tp"), None)
    return jax.shard_map(
        per_device,
        mesh=mesh,
        in_specs=(split, split, split, split, P()),
        out_specs=(split, split, split),
        check_vma=False,
    )
```

```python
import itertools
import math

import jax
import jax.numpy as jnp
from jax import lax
from jax.experimental import pallas as pl
from jax.experimental.pallas import tpu as pltpu
from jax.sharding import PartitionSpec as P

QUERY_HEADS = 32
KEY_HEADS = 16
HEAD_SIZE = 128
WINDOW = 1024
GROUP = QUERY_HEADS // KEY_HEADS
AXES = ("seq", "tp")

attn_scale = 168.0 ** (-0.5)
masked_floor = -1e30

CHUNKS = 2
EASY, HARD = 1 << 21, 1 << 25
VMEM_LIMIT = 56 * 1024 * 1024
ANY = pl.BlockSpec(memory_space=pl.ANY)
VMEM = pl.BlockSpec(memory_space=pltpu.VMEM)
SMEM = pl.BlockSpec(memory_space=pltpu.SMEM)


class Plan:
    def __init__(self, rows):
        self.seq, self.tp = lax.axis_size("seq"), lax.axis_size("tp")
        self.rows = rows
        self.block = rows * self.tp
        self.slab = WINDOW // self.block
        self.cores = min(2, self.slab)
        self.ways = self.slab // self.cores
        self.groups = self.ways * self.tp
        self.key_heads = KEY_HEADS // self.groups
        self.chunks = min(CHUNKS, self.key_heads)
        self.heads = self.key_heads // self.chunks
        self.key_cols = self.heads * HEAD_SIZE
        self.query_cols = self.key_cols * GROUP
        self.pieces = self.slab * self.tp
        self.flips = sorted(range(self.groups), key=lambda flip: (flip > 0, -bin(flip).count("1")))

    def place(self):
        seq, tp = lax.axis_index("seq"), lax.axis_index("tp")
        inner = lax.rem(seq, self.slab)
        core = lax.rem(inner, self.cores)
        return seq - inner, core, (inner // self.cores) * self.tp + tp

    def routes(self, move):
        pairs = []
        for seq in range(self.seq):
            for tp in range(self.tp):
                slab, inner = divmod(seq, self.slab)
                way, core = divmod(inner, self.cores)
                to_slab, to_core, to_group = move(slab, core, way * self.tp + tp)
                to_slab %= self.seq // self.slab
                target = (to_slab * self.slab + to_group // self.tp * self.cores + to_core) * self.tp + to_group % self.tp
                pairs.append((seq * self.tp + tp, target))
        return pairs

    def to_group(self, value, flip):
        return lax.ppermute(value, AXES, self.routes(lambda slab, core, group: (slab, core, group ^ flip)))

    def to_core(self, value):
        return lax.ppermute(value, AXES, self.routes(lambda slab, core, group: (slab, self.cores - 1 - core, group)))

    def to_slab(self, value, step):
        return lax.ppermute(value, AXES, self.routes(lambda slab, core, group: (slab + step, core, group)))


def run_copies(copies):
    for copy in copies:
        copy.start()
    for copy in copies:
        copy.wait()


def traffic(count):
    return pl.CostEstimate(flops=0, bytes_accessed=count, transcendentals=0)


def columns(start, width):
    return pl.ds(pl.multiple_of(start, HEAD_SIZE), width)


def split_columns(plan, arrays, width, chunks, name, after=()):
    chunk_width = width // chunks

    def kernel(*refs):
        sources, targets, sem = refs[: len(arrays)], refs[len(arrays) + len(after) : -1], refs[-1]
        _, _, group = plan.place()
        copies = []
        for chunk in range(chunks):
            for at, flip in enumerate(plan.flips):
                start = (group ^ flip) * width + chunk * chunk_width
                for index, source in enumerate(sources):
                    copies.append(
                        pltpu.make_async_copy(
                            source.at[:, columns(start, chunk_width)],
                            targets[chunk * plan.groups + at].at[index],
                            sem.at[len(copies)],
                        )
                    )
        run_copies(copies)

    count = chunks * plan.groups
    shape = jax.ShapeDtypeStruct((len(arrays), plan.rows, chunk_width), jnp.bfloat16)
    out = pl.pallas_call(
        kernel,
        out_shape=[shape] * count,
        in_specs=[ANY] * (len(arrays) + len(after)),
        out_specs=[VMEM] * count,
        scratch_shapes=[pltpu.SemaphoreType.DMA((count * len(arrays),))],
        cost_estimate=traffic(2 * sum(array.nbytes for array in arrays)),
        name=name,
    )(*arrays, *after)
    return [out[chunk * plan.groups : (chunk + 1) * plan.groups] for chunk in range(chunks)]


def ordered(value, cost, after):
    def kernel(*refs):
        pass

    return pl.pallas_call(
        kernel,
        out_shape=jax.ShapeDtypeStruct(value.shape, value.dtype),
        in_specs=[ANY] * (1 + len(after)),
        out_specs=ANY,
        input_output_aliases={0: 0},
        cost_estimate=traffic(cost),
        name="ordered",
    )(value, *after)


def backward(plan, chunk, doc_lengths, query_pieces, key_arrays, earlier, after):
    tiles = plan.slab + 1
    block, groups, tp, cores = plan.block, plan.groups, plan.tp, plan.cores
    heads, key_cols, query_cols = plan.heads, plan.key_cols, plan.query_cols
    wide = GROUP * block
    query_width = HEAD_SIZE * GROUP
    exponent_scale = attn_scale * math.log2(math.e)
    loads = heads * 5 * groups
    stores = heads * (2 * groups + 3) + len(earlier)

    def kernel(docs, *refs):
        pieces, refs = refs[:groups], refs[groups:]
        key_refs, refs = refs[:4], refs[4:]
        early, refs = refs[: len(earlier)], refs[len(earlier) + len(after) :]
        query_out, refs = refs[:groups], refs[groups:]
        before_mine, own_mine, own_far, refs = *refs[:3], refs[3:]
        parts = (before_mine, None, own_mine, own_far)
        before_far, refs = refs[:groups], refs[groups:]
        qo_s, kv_s, dq_s, early_s, dk_s, dv_s, part_s, score_s, prob_grad_s, prob_s, grad_s, sem, out_sem = refs
        q_s, o_s, k_s, v_s = qo_s.at[0], qo_s.at[1], kv_s.at[0], kv_s.at[1]
        slab_seq, core, group = plan.place()

        copies, results = [], []

        def block_of(late, away, flip):
            side = core + away * (cores - 1 - 2 * core)
            return late * plan.pieces + ((group ^ flip) // tp * cores + side) * tp + lax.rem(group ^ flip, tp)

        def load(source, target):
            copies.append(pltpu.make_async_copy(source, target, sem.at[len(copies)]))
            copies[-1].start()

        def store(source, target):
            results.append(pltpu.make_async_copy(source, target, out_sem.at[len(results)]))
            results[-1].start()

        for head in range(heads):
            here, there = pl.ds(head * query_width, query_width), pl.ds((chunk * heads + head) * query_width, query_width)
            for flip, piece in zip(plan.flips, pieces):
                load(piece.at[:, :, there], qo_s.at[:, group ^ flip, :, here])
            here, there = pl.ds(head * HEAD_SIZE, HEAD_SIZE), pl.ds((chunk * heads + head) * HEAD_SIZE, HEAD_SIZE)
            for source, (late, away) in zip(key_refs, itertools.product((1, 0), (0, 1))):
                for at, flip in enumerate(plan.flips):
                    load(source.at[at, :, :, there], kv_s.at[:, block_of(late, away, flip), :, here])
        for at, source in enumerate(early):
            load(source, early_s.at[at])
        dk_s[...] = jnp.zeros_like(dk_s)
        dv_s[...] = jnp.zeros_like(dv_s)

        def step(head, way):
            key_at = (way * cores + core) * tp
            head_cols = pl.ds(head * HEAD_SIZE, HEAD_SIZE)
            rows_at = pl.ds(way * tp, tp)

            def both(ref):
                parts = [
                    ref[rows_at, :, pl.ds((head * GROUP + member) * HEAD_SIZE, HEAD_SIZE)].reshape(block, HEAD_SIZE)
                    for member in range(GROUP)
                ]
                return jnp.concatenate(parts, axis=0)

            queries, grads = both(q_s), both(o_s)
            inner = lax.broadcasted_iota(jnp.int32, (1, block), 1)
            inner = jnp.concatenate([inner] * GROUP, axis=1)
            first = (slab_seq + way * cores + core) * block
            position = inner + first
            lowest = position - (WINDOW - 1)
            start = jnp.int32(0)
            for doc in range(docs.shape[0]):
                lowest = jnp.where(position >= start, jnp.maximum(lowest, start), lowest)
                start = start + docs[doc]
            lowest = lowest - (first - WINDOW)

            def key_rows(ref, tile):
                return ref[pl.ds(key_at + tile * tp, tp), :, head_cols].reshape(block, HEAD_SIZE)

            def tile_rows(tile):
                return pl.ds(tile * block, block)

            peak = jnp.full((1, wide), masked_floor, jnp.float32)
            for tile in range(tiles):
                scores = lax.dot_general(
                    key_rows(k_s, tile), queries, (((1,), (1,)), ((), ())), preferred_element_type=jnp.float32
                )
                row = lax.broadcasted_iota(jnp.int32, (block, wide), 0)
                allowed = row >= lowest - tile * block
                if tile == tiles - 1:
                    allowed = allowed & (row <= inner)
                scores = jnp.where(allowed, scores, masked_floor)
                peak = jnp.maximum(peak, jnp.max(scores, axis=0, keepdims=True))
                score_s[tile_rows(tile), :] = scores
            peak = peak * exponent_scale
            total = jnp.zeros((1, wide), jnp.float32)
            delta = jnp.zeros((1, wide), jnp.float32)
            for tile in range(tiles):
                raised = jnp.exp2(score_s[tile_rows(tile), :] * exponent_scale - peak)
                prob_grad = lax.dot_general(
                    key_rows(v_s, tile), grads, (((1,), (1,)), ((), ())), preferred_element_type=jnp.float32
                )
                total = total + jnp.sum(raised, axis=0, keepdims=True)
                score_s[tile_rows(tile), :] = raised
                prob_grad_s[tile_rows(tile), :] = prob_grad
            inverse = 1.0 / total
            for tile in range(tiles):
                rounded = (score_s[tile_rows(tile), :] * inverse).astype(jnp.bfloat16)
                prob_s[tile_rows(tile), :] = rounded
                product = rounded.astype(jnp.float32) * prob_grad_s[tile_rows(tile), :]
                delta = delta + jnp.sum(product, axis=0, keepdims=True)
            for tile in range(tiles):
                probs = score_s[tile_rows(tile), :] * inverse
                grad_scores = probs * (prob_grad_s[tile_rows(tile), :] - delta) * attn_scale
                grad_s[tile_rows(tile), :] = grad_scores.astype(jnp.bfloat16)
            at = pl.ds(key_at, tiles * tp)
            shape = (tiles * tp, plan.rows, HEAD_SIZE)
            dv_s[at, :, head_cols] += jnp.dot(prob_s[...], grads, preferred_element_type=jnp.float32).reshape(shape)
            dk_s[at, :, head_cols] += jnp.dot(grad_s[...], queries, preferred_element_type=jnp.float32).reshape(shape)
            query_sum = lax.dot_general(
                k_s[at, :, head_cols].reshape(tiles * block, HEAD_SIZE),
                grad_s[...],
                (((0,), (0,)), ((), ())),
                preferred_element_type=jnp.float32,
            )
            query_rows = query_sum.T.astype(jnp.bfloat16)
            for member in range(GROUP):
                dq_s[rows_at, :, pl.ds((head * GROUP + member) * HEAD_SIZE, HEAD_SIZE)] = query_rows[
                    member * block : (member + 1) * block
                ].reshape(tp, plan.rows, HEAD_SIZE)

        for head in range(heads):
            for copy in copies[head * loads // heads : (head + 1) * loads // heads]:
                copy.wait()
            for way in range(plan.ways):
                step(head, way)
            if head == 0:
                for copy in copies[loads:]:
                    copy.wait()
                for at, target in enumerate(query_out[: len(early)]):
                    store(early_s.at[at], target.at[pl.ds(0, chunk)])
            head_cols = pl.ds(head * HEAD_SIZE, HEAD_SIZE)
            for late, away in itertools.product((0, 1), (0, 1)):
                staged = part_s.at[late, away]
                for (at, flip), index in itertools.product(enumerate(plan.flips), (0, 1)):
                    total = (dk_s, dv_s)[index][block_of(late, away, flip), :, head_cols]
                    staged[at, index, :, head_cols] = total.astype(jnp.bfloat16)
                if late or not away:
                    store(staged.at[:, :, :, head_cols], parts[2 * late + away].at[:, :, :, head_cols])
                else:
                    for piece in range(groups):
                        store(staged.at[piece, :, :, head_cols], before_far[piece].at[:, :, head_cols])
            done_part = pl.ds(head * query_width, query_width)
            for at, flip in enumerate(plan.flips):
                store(dq_s.at[group ^ flip, :, done_part], query_out[at].at[chunk, :, done_part])
        for copy in results:
            copy.wait()

    part = (groups, 2, plan.rows, key_cols)
    bf, fl = jnp.bfloat16, jnp.float32
    span = 2 * plan.pieces
    pairs = tiles * block * wide * heads * plan.ways
    out = pl.pallas_call(
        kernel,
        out_shape=[jax.ShapeDtypeStruct((chunk + 1, plan.rows, query_cols), bf)] * groups
        + [jax.ShapeDtypeStruct(part, bf)] * 3
        + [jax.ShapeDtypeStruct(part[1:], bf)] * groups,
        in_specs=[SMEM] + [ANY] * (groups + 4 + len(earlier) + len(after)),
        out_specs=[ANY] * (2 * groups + 3),
        scratch_shapes=[
            pltpu.VMEM((2, groups, plan.rows, query_cols), bf),
            pltpu.VMEM((2, span, plan.rows, key_cols), bf),
            pltpu.VMEM((groups, plan.rows, query_cols), bf),
            pltpu.VMEM((groups, max(chunk, 1), plan.rows, query_cols), bf),
            pltpu.VMEM((span, plan.rows, key_cols), fl),
            pltpu.VMEM((span, plan.rows, key_cols), fl),
            pltpu.VMEM((2, 2) + part, bf),
            pltpu.VMEM((tiles * block, wide), fl),
            pltpu.VMEM((tiles * block, wide), fl),
            pltpu.VMEM((tiles * block, wide), bf),
            pltpu.VMEM((tiles * block, wide), bf),
            pltpu.SemaphoreType.DMA((loads + len(earlier),)),
            pltpu.SemaphoreType.DMA((stores,)),
        ],
        compiler_params=pltpu.CompilerParams(vmem_limit_bytes=VMEM_LIMIT),
        cost_estimate=pl.CostEstimate(flops=160 * pairs * HEAD_SIZE, bytes_accessed=6 << 20, transcendentals=pairs),
        name="backward",
    )(doc_lengths, *query_pieces, *key_arrays, *earlier, *after)
    return out[:groups], out[groups : groups + 3], out[groups + 3 :]


def token(arrays):
    return sum(array.reshape(-1, array.shape[-1])[:16, :HEAD_SIZE] for array in arrays)


def add_up(*parts):
    total = parts[0].astype(jnp.float32)
    for part in parts[1:]:
        total = total + part.astype(jnp.float32)
    return total.astype(jnp.bfloat16)


def join_columns(plan, sources, targets, width, name):
    flat = [piece for pieces in sources for piece in pieces[::-1]]
    chunks = len(targets[0])
    chunk_width = width // chunks

    def kernel(*refs):
        pieces, outs, sem = refs[: len(flat)], refs[len(flat) : -1], refs[-1]
        _, _, group = plan.place()
        copies = []
        for out, parts in zip(outs, targets):
            for chunk, (which, row, column) in enumerate(parts):
                for at, flip in enumerate(plan.flips):
                    start = (group ^ flip) * width + chunk * chunk_width
                    copies.append(
                        pltpu.make_async_copy(
                            pieces[(which + 1) * plan.groups - 1 - at].at[row, :, pl.ds(column, chunk_width)],
                            out.at[:, columns(start, chunk_width)],
                            sem.at[len(copies)],
                        )
                    )
        run_copies(copies)

    return pl.pallas_call(
        kernel,
        out_shape=[jax.ShapeDtypeStruct((plan.rows, width * plan.groups), jnp.bfloat16)] * len(targets),
        in_specs=[ANY] * len(flat),
        out_specs=[VMEM] * len(targets),
        scratch_shapes=[pltpu.SemaphoreType.DMA((len(targets) * chunks * plan.groups,))],
        cost_estimate=traffic(2 * sum(piece.nbytes for piece in flat)),
        name=name,
    )(*flat)


def per_device(queries, key_states, value_state_rows, out_grad, doc_lengths):
    plan = Plan(queries.shape[0])
    key_width = KEY_HEADS * HEAD_SIZE // plan.groups
    query_width = QUERY_HEADS * HEAD_SIZE // plan.groups

    def exchange(pieces):
        return [pieces[0]] + [plan.to_group(piece, flip) for piece, flip in zip(pieces[1:], plan.flips[1:])]

    key_parts = split_columns(plan, (key_states, value_state_rows), key_width, 1, "split_keys")[0]
    query_parts = split_columns(plan, (queries, out_grad), query_width, 1, "split_queries", after=(key_parts[0],))[0]
    pieces = exchange(key_parts)
    arrived = exchange(query_parts)
    own_first = ordered(pieces[0], HARD, pieces[1:])
    own = jnp.stack([own_first, *pieces[1:]])
    own_other = plan.to_core(own)
    moved = [plan.to_slab(pieces[0], 1), plan.to_slab(pieces[1], 1)]
    if plan.groups > 2:
        rest = plan.to_slab(jnp.stack(pieces[2:]), 1)
        moved = moved + [rest[at] for at in range(plan.groups - 2)]
    before = jnp.stack([ordered(moved[0], HARD, (own_first, *arrived[1:])), *moved[1:]])
    before_other = plan.to_core(before)
    key_arrays = (own, own_other, before, before_other)
    after, hold, query_out = (), (), ()
    sums = []
    for chunk in range(plan.chunks):
        query_out, (before_mine, own_mine, own_far), before_far = backward(
            plan, chunk, doc_lengths, arrived, key_arrays, query_out, after
        )
        if hold:
            before_mine = ordered(before_mine, EASY, hold)
        before_sum = add_up(before_mine, jnp.stack([plan.to_core(piece) for piece in before_far]))
        later = plan.to_slab(before_sum, -1)
        sums.append((own_mine, plan.to_core(own_far), later))
        after, hold = (token((before_sum,)),), (later,)
    query_sent = exchange(query_out)
    key_sent = []
    for chunk, (own_mine, own_far, later) in enumerate(sums):
        if chunk < plan.chunks - 1:
            own_mine = ordered(own_mine, HARD, query_out[:1])
        key_sent.append(exchange([add_up(own_mine[at], own_far[at], later[at]) for at in range(plan.groups)]))
    chunks = range(plan.chunks)
    (query_grad,) = join_columns(plan, [query_sent], [[(0, chunk, 0) for chunk in chunks]], query_width, "join_queries")
    key_gradient, value_gradient = join_columns(
        plan, key_sent, [[(chunk, index, 0) for chunk in chunks] for index in (0, 1)], key_width, "join_keys"
    )
    return query_grad, key_gradient, value_gradient


def solution(mesh):
    split = P(("seq", "tp"), None)
    return jax.shard_map(
        per_device,
        mesh=mesh,
        in_specs=(split, split, split, split, P()),
        out_specs=(split, split, split),
        check_vma=False,
    )
```
